32 devices in a mesh: tok: 8 (over z, y), tp: 4 (over x, core).
Axes of the slice: x: 2, y: 2, z: 4, core: 2. Of those that a mesh axis runs over, the one named last changes fastest.
Arguments:
- inputs: bfloat16 [6144, 2304], P('tok'), may hold values from -7 to 7
- seq_lengths: int32 [4], replicated, may hold values from 1024 to 2048, as said below
- gain_attn_in: bfloat16 [2304], P('tok'), may hold values from 0.5 to 1.5
- gain_attn_out: bfloat16 [2304], P('tok'), may hold values from 0.5 to 1.5
- gain_ffn_in: bfloat16 [2304], P('tok'), may hold values from 0.5 to 1.5
- gain_ffn_out: bfloat16 [2304], P('tok'), may hold values from 0.5 to 1.5
- w_query: bfloat16 [2304, 2048], P('tok', 'tp'), may hold values from -2 to 2
- w_key: bfloat16 [2304, 1024], P('tok', 'tp'), may hold values from -2 to 2
- w_value: bfloat16 [2304, 1024], P('tok', 'tp'), may hold values from -0.125 to 0.125
- w_out: bfloat16 [2304, 2048], P('tok', 'tp'), may hold values from -0.125 to 0.125
- w_gate: bfloat16 [2304, 9216], P('tok', 'tp'), may hold values from -0.125 to 0.125
- w_up: bfloat16 [2304, 9216], P('tok', 'tp'), may hold values from -0.125 to 0.125
- w_down: bfloat16 [2304, 9216], P('tok', 'tp'), may hold values from -0.0625 to 0.0625
- out_grad: bfloat16 [6144, 2304], P('tok'), may hold values from -6 to 6
Outputs:
- layer_out: bfloat16 [6144, 2304], P('tok')
- input_grad: float32 [6144, 2304], P('tok')
- gain_attn_in_grad: float32 [2304], P('tok')
- gain_attn_out_grad: float32 [2304], P('tok')
- gain_ffn_in_grad: float32 [2304], P('tok')
- gain_ffn_out_grad: float32 [2304], P('tok')
- w_query_grad: float32 [2304, 2048], P('tok', 'tp')
- w_key_grad: float32 [2304, 1024], P('tok', 'tp')
- w_value_grad: float32 [2304, 1024], P('tok', 'tp')
- w_out_grad: float32 [2304, 2048], P('tok', 'tp')
- w_gate_grad: float32 [2304, 9216], P('tok', 'tp')
- w_up_grad: float32 [2304, 9216], P('tok', 'tp')
- w_down_grad: float32 [2304, 9216], P('tok', 'tp')
The draws below stay inside these ranges and needn't reach their ends.
Inputs may be any that keep to these rules, and one draw needn't show every extreme that they name: `seq_lengths`: lengths of the 4 packed sequences in order; they sum to 6144, and entries 2k and 2k + 1 sum to 3072.
All inputs are finite; a program needn't handle non-finite values.
Results may differ from the reference program's by a relative error of at most 0.023.
Values may be sent and summed in bfloat16 or wider, within the bound.
A program may use at most 256 MiB of HBM per device.

```python
import math
import jax
import jax.numpy as jnp
from jax import lax

WIDTH = 2304
HEADS = 8
KV_HEADS = 4
HEAD_DIM = 256
HIDDEN_SIZE = 9216
TOK_DEV = 768
MAX_LEN = 2048
MIN_LEN = 1024
TOKENS = 6144
SEQS = 4
REACH = 3


def draw_seq_lengths(key, part):
    pairs = SEQS // 2
    leading = jax.random.randint(jax.random.fold_in(key, 11), (pairs,), MIN_LEN, MAX_LEN + 1)
    chosen = jax.random.randint(jax.random.fold_in(key, 12), (), 0, pairs)
    leading = jnp.where(jnp.arange(pairs) == chosen, MAX_LEN, leading)
    flipped = jax.random.randint(jax.random.fold_in(key, 13), (pairs,), 0, 2)
    partner = MAX_LEN + MIN_LEN - leading
    front_len = jnp.where(flipped == 1, leading, partner)
    back_len = jnp.where(flipped == 1, partner, leading)
    return jnp.stack([front_len, back_len], axis=1).reshape(SEQS).astype(jnp.int32)


def shared_direction(key):
    return jax.random.truncated_normal(jax.random.fold_in(key, 501), -3.0, 3.0, (WIDTH,), jnp.float32)


def draw_inputs(key, part):
    noise_part = jax.random.truncated_normal(jax.random.fold_in(key, 502), -4.0, 4.0, (TOKENS, WIDTH), jnp.float32)
    return (shared_direction(key)[None, :] + noise_part).astype(jnp.bfloat16)


def drawn_columns(head_count):
    pair_count = max(1, HEAD_DIM // 64)
    half_dim = HEAD_DIM // 2
    within = jnp.arange(head_count * HEAD_DIM) % HEAD_DIM
    chosen = (within >= half_dim - pair_count) & (within < half_dim) | (within >= HEAD_DIM - pair_count)
    return chosen.astype(jnp.float32)


def drawn_weight(key, head_count, lowest, topmost, seed_salt):
    noise_part = jax.random.truncated_normal(jax.random.fold_in(key, seed_salt), -4.0, 4.0, (WIDTH, head_count * HEAD_DIM), jnp.float32) * WIDTH ** (-0.5)
    strength = jnp.exp(jax.random.uniform(jax.random.fold_in(key, seed_salt + 1), (head_count,), jnp.float32, math.log(lowest), math.log(topmost)))
    per_column = jnp.repeat(strength, HEAD_DIM) * drawn_columns(head_count)
    common_part = shared_direction(key)[:, None] * per_column[None, :] * (math.sqrt(2.0) / WIDTH)
    return (noise_part + common_part).astype(jnp.bfloat16)


def draw_w_query(key, part):
    return drawn_weight(key, HEADS, 5.0, 14.0, 601)


def draw_w_key(key, part):
    return drawn_weight(key, KV_HEADS, 4.5, 5.5, 701)


def block_levels(own_key, extent, split, least, largest):
    def one(dim, shards_of):
        draws = jax.random.uniform(jax.random.fold_in(jax.random.fold_in(own_key, 6), dim), (shards_of,), jnp.float32, least / len(split), largest / len(split))
        return jnp.repeat(jnp.exp(draws), extent[dim] // shards_of).reshape((-1,) + (1,) * (len(extent) - dim - 1))

    loudness = one(*split[0])
    for cut in split[1:]:
        loudness = loudness * one(*cut)
    return loudness


def scatter_about(rng, dims, width, most, shards=(), dtype=jnp.bfloat16):
    level = block_levels(rng, dims, shards, -0.22, 0.18) if shards else 1.0
    values = jax.random.normal(rng, dims, jnp.float32) * width * level
    return jnp.minimum(jnp.maximum(values, -most), most).astype(dtype)


def setup_inputs(seed: int = 0) -> dict:
    seeds = jax.random.split(jax.random.key(seed), 15)
    return {
        "inputs": draw_inputs(jax.random.fold_in(seeds[14], 71), 0),
        "seq_lengths": draw_seq_lengths(jax.random.fold_in(seeds[14], 71), 0),
        "gain_attn_in": jnp.clip(1.0 + 0.1 * jax.random.normal(seeds[2], (WIDTH,), jnp.float32), 0.5, 1.5).astype(jnp.bfloat16),
        "gain_attn_out": jnp.clip(1.0 + 0.1 * jax.random.normal(seeds[3], (WIDTH,), jnp.float32), 0.5, 1.5).astype(jnp.bfloat16),
        "gain_ffn_in": jnp.clip(1.0 + 0.1 * jax.random.normal(seeds[4], (WIDTH,), jnp.float32), 0.5, 1.5).astype(jnp.bfloat16),
        "gain_ffn_out": jnp.clip(1.0 + 0.1 * jax.random.normal(seeds[5], (WIDTH,), jnp.float32), 0.5, 1.5).astype(jnp.bfloat16),
        "w_query": draw_w_query(jax.random.fold_in(seeds[14], 71), 0),
        "w_key": draw_w_key(jax.random.fold_in(seeds[14], 71), 0),
        "w_value": scatter_about(seeds[8], (WIDTH, KV_HEADS * HEAD_DIM), WIDTH ** -0.5, 0.125, ((0, 8), (1, 4))),
        "w_out": scatter_about(seeds[9], (WIDTH, HEADS * HEAD_DIM), (HEADS * HEAD_DIM) ** -0.5, 0.125, ((0, 8), (1, 4))),
        "w_gate": scatter_about(seeds[10], (WIDTH, HIDDEN_SIZE), WIDTH ** -0.5, 0.125, ((0, 8), (1, 4))),
        "w_up": scatter_about(seeds[11], (WIDTH, HIDDEN_SIZE), WIDTH ** -0.5, 0.125, ((0, 8), (1, 4))),
        "w_down": scatter_about(seeds[12], (WIDTH, HIDDEN_SIZE), HIDDEN_SIZE ** -0.5, 0.0625, ((0, 8), (1, 4))),
        "out_grad": scatter_about(seeds[13], (TOKENS, WIDTH), 1.0, 6.0, ((0, 8),)),
    }


@jax.custom_vjp
def low(v):
    return lax.optimization_barrier(v.astype(jnp.bfloat16)).astype(jnp.float32)

@jax.custom_vjp
def low_back(v):
    return v

def low_keep(v):
    return (low(v), None)

def low_pass(kept, grad):
    return (grad,)

def back_keep(v):
    return (v, None)

def back_low(kept, grad):
    return (low(grad),)
low.defvjp(low_keep, low_pass)
low_back.defvjp(back_keep, back_low)
softcap_limit = 50.0
norm_epsilon = 1e-06
rope_base = 10000.0
negative_fill = -1e+30
highest = lax.Precision.HIGHEST

def norm_scale(values, gain_vec):
    return values * lax.rsqrt(lax.optimization_barrier(jnp.mean(values * values, axis=-1, keepdims=True)) + norm_epsilon) * gain_vec

def token_places(seq_lengths, tok_index):
    starts = (jnp.cumsum(seq_lengths) - seq_lengths).astype(jnp.int32)
    passed = tok_index[:, None] >= starts[None, :]
    segment = (lax.optimization_barrier(jnp.sum(passed.astype(jnp.int32), axis=1)) - 1).astype(jnp.int32)
    seq_start = lax.optimization_barrier(jnp.max(jnp.where(passed, starts[None, :], 0), axis=1)).astype(jnp.int32)
    return (segment, (tok_index - seq_start).astype(jnp.int32))

def rope_tables(position):
    half_dim = HEAD_DIM // 2
    freqs = rope_base ** (-2.0 * jnp.arange(half_dim).astype(jnp.float32) / HEAD_DIM)
    theta = position.astype(jnp.float32)[:, None] * freqs[None, :]
    return (jnp.cos(theta)[:, None, :], jnp.sin(theta)[:, None, :])

def rotate(values, cosine, sine_tab):
    half_dim = values.shape[-1] // 2
    front_half = values[..., :half_dim]
    back_half = values[..., half_dim:]
    return jnp.concatenate([front_half * cosine - back_half * sine_tab, back_half * cosine + front_half * sine_tab], axis=-1)

def matmul(left, right):
    return jnp.dot(left, right, precision=highest, preferred_element_type=jnp.float32)

def forward(resid, gain_one, gain_two, gain_three, gain_four, w_query, w_key, w_value, w_out, w_gate, w_up, w_down, segment, position):
    count = resid.shape[0]
    group = HEADS // KV_HEADS
    score_scale = HEAD_DIM ** (-0.5)
    reach_rows = REACH * TOK_DEV
    window = reach_rows + TOK_DEV
    hidden_one = low(norm_scale(resid, gain_one))
    query = low_back(matmul(hidden_one, w_query))
    key_pre = low_back(matmul(hidden_one, w_key))
    value_vec = low(low_back(matmul(hidden_one, w_value))).reshape(count, KV_HEADS, HEAD_DIM)
    cosine, sine_tab = rope_tables(position)
    query_rot = low(rotate(query.reshape(count, HEADS, HEAD_DIM), cosine, sine_tab))
    key_rot = low(rotate(key_pre.reshape(count, KV_HEADS, HEAD_DIM), cosine, sine_tab))
    key_pad = jnp.concatenate([jnp.zeros((reach_rows, KV_HEADS, HEAD_DIM), jnp.float32), key_rot], axis=0)
    value_pad = jnp.concatenate([jnp.zeros((reach_rows, KV_HEADS, HEAD_DIM), jnp.float32), value_vec], axis=0)
    seg_pad = jnp.concatenate([jnp.full((reach_rows,), -1, jnp.int32), segment], axis=0)
    pos_pad = jnp.concatenate([jnp.zeros((reach_rows,), jnp.int32), position], axis=0)

    def block_attend(block_start):
        query_blk = lax.dynamic_slice_in_dim(query_rot, block_start, TOK_DEV, 0).reshape(TOK_DEV, KV_HEADS, group, HEAD_DIM)
        key_blk = lax.dynamic_slice_in_dim(key_pad, block_start, window, 0)
        value_blk = lax.dynamic_slice_in_dim(value_pad, block_start, window, 0)
        seg_query = lax.dynamic_slice_in_dim(segment, block_start, TOK_DEV, 0)
        pos_query = lax.dynamic_slice_in_dim(position, block_start, TOK_DEV, 0)
        seg_key = lax.dynamic_slice_in_dim(seg_pad, block_start, window, 0)
        pos_key = lax.dynamic_slice_in_dim(pos_pad, block_start, window, 0)
        allowed = (seg_query[:, None] == seg_key[None, :]) & (pos_key[None, :] <= pos_query[:, None])
        raw_scores = low_back(jnp.einsum('qgjd,kgd->gjqk', query_blk, key_blk, precision=highest))
        capped = softcap_limit * jnp.tanh(raw_scores * score_scale / softcap_limit)
        masked = jnp.where(allowed[None, None], capped, negative_fill)
        row_max = lax.optimization_barrier(jnp.max(masked, axis=-1, keepdims=True))
        exponent = jnp.exp(masked - row_max)
        probs = low(exponent / lax.optimization_barrier(jnp.sum(exponent, axis=-1, keepdims=True)))
        mixed = jnp.einsum('gjqk,kgd->qgjd', probs, value_blk, precision=highest)
        return mixed.reshape(TOK_DEV, HEADS * HEAD_DIM)
    block_starts = (jnp.arange(count // TOK_DEV) * TOK_DEV).astype(jnp.int32)
    attended = lax.map(jax.checkpoint(block_attend), block_starts).reshape(count, HEADS * HEAD_DIM)
    attended = low(low_back(attended))
    attn = low_back(matmul(attended, w_out.T))
    mid = resid + norm_scale(attn, gain_two)
    hidden_two = low(norm_scale(mid, gain_three))
    gate = low_back(matmul(hidden_two, w_gate))
    up_vals = low_back(matmul(hidden_two, w_up))
    inner = low(jax.nn.gelu(gate, approximate=True) * up_vals)
    ffn = low_back(matmul(inner, w_down.T))
    return mid + norm_scale(ffn, gain_four)

def reference(inputs, seq_lengths, gain_attn_in, gain_attn_out, gain_ffn_in, gain_ffn_out, w_query, w_key, w_value, w_out, w_gate, w_up, w_down, out_grad):
    tok_index = jnp.arange(TOKENS).astype(jnp.int32)
    segment, position = token_places(seq_lengths.astype(jnp.int32), tok_index)
    floats = tuple((entry.astype(jnp.float32) for entry in (inputs, gain_attn_in, gain_attn_out, gain_ffn_in, gain_ffn_out, w_query, w_key, w_value, w_out, w_gate, w_up, w_down)))

    def apply_layer(*params):
        return forward(*params, segment, position)
    result, pull_back = jax.vjp(apply_layer, *floats)
    grads_all = pull_back(out_grad.astype(jnp.float32))
    return (result.astype(jnp.bfloat16), grads_all[0], grads_all[1], grads_all[2], grads_all[3], grads_all[4], grads_all[5], grads_all[6], grads_all[7], grads_all[8], grads_all[9], grads_all[10], grads_all[11])
```

```python
from functools import partial

import jax
import jax.numpy as jnp
from jax import lax
from jax.sharding import PartitionSpec as P

HEAD_DIM = 256
QUAD = 4
REACH = 2

softcap_limit = 50.0
norm_epsilon = 1e-06
rope_base = 10000.0
negative_fill = -1e30

f32 = jnp.float32
bf16 = jnp.bfloat16


def norm_parts(values):
    inverse = lax.rsqrt(jnp.mean(values * values, axis=-1, keepdims=True) + norm_epsilon)
    return values * inverse, inverse


def norm_back(gradient, gain_vec, unit_vals, inverse):
    scaled = gradient * gain_vec
    input_part = inverse * (
        scaled - unit_vals * jnp.mean(scaled * unit_vals, axis=-1, keepdims=True)
    )
    return (input_part, jnp.sum(gradient * unit_vals, axis=0))


def token_places(seq_lengths, tok_index):
    count = seq_lengths.shape[0]
    before = jnp.arange(count)[:, None] > jnp.arange(count)[None, :]
    starts = jnp.sum(jnp.where(before, seq_lengths[None, :], 0), axis=1)
    passed = tok_index[:, None] >= starts[None, :]
    segment = jnp.sum(passed.astype(jnp.int32), axis=1) - 1
    seq_start = jnp.max(jnp.where(passed, starts[None, :], 0), axis=1)
    return (segment, tok_index - seq_start)


def rope_tables(position):
    half_dim = HEAD_DIM // 2
    freqs = rope_base ** (-2.0 * jnp.arange(half_dim).astype(f32) / HEAD_DIM)
    theta = position.astype(f32)[:, None] * freqs[None, :]
    return (jnp.cos(theta)[:, None, :], jnp.sin(theta)[:, None, :])


def rotate(values, cosine, sine_tab):
    half_dim = values.shape[-1] // 2
    front_half = values[..., :half_dim]
    back_half = values[..., half_dim:]
    return jnp.concatenate(
        [front_half * cosine - back_half * sine_tab, back_half * cosine + front_half * sine_tab],
        axis=-1,
    )


def contract_rows(left, right):
    return lax.dot_general(
        left, right, (((0,), (0,)), ((), ())), preferred_element_type=f32
    )


def contract_cols(left, right):
    return lax.dot_general(
        left, right, (((1,), (1,)), ((), ())), preferred_element_type=f32
    )


def pick(array, index, axis=0):
    return lax.dynamic_index_in_dim(array, index, axis, keepdims=False)


def put(buffer, block, index):
    return lax.dynamic_update_index_in_dim(buffer, block, index, 0)


def local(
    inputs,
    seq_lengths,
    gain_attn_in,
    gain_attn_out,
    gain_ffn_in,
    gain_ffn_out,
    w_query,
    w_key,
    w_value,
    w_out,
    w_gate,
    w_up,
    w_down,
    out_grad,
):
    n = lax.axis_size("tok")
    m = n // 4
    width = inputs.shape[1]
    rows = inputs.shape[0]
    part = rows // 4
    tok = lax.axis_index("tok")
    tpi = lax.axis_index("tp")
    z, y = tok // m, tok % m
    zlo, zhi = z % 2, z // 2
    x, core = tpi // 2, tpi % 2
    wrows = w_query.shape[0]
    head_cols = w_query.shape[1]
    kv_cols = w_key.shape[1]
    heads = head_cols // HEAD_DIM
    units = w_gate.shape[1]
    half = units // 2

    def over_tok(fn):
        pairs = [(t, fn(t)) for t in range(n)]
        return lambda a: lax.ppermute(a, "tok", pairs)

    def over_tp(fn):
        pairs = [(t, fn(t)) for t in range(4)]
        return lambda a: lax.ppermute(a, "tp", pairs)

    def z_shift(a, k):
        return over_tok(lambda t: ((t // m + k) % 4) * m + t % m)(a)

    def y_shift(a, k):
        return over_tok(lambda t: (t // m) * m + (t % m + k) % m)(a)

    to_zlo = over_tok(lambda t: ((t // m) ^ 1) * m + t % m)
    to_zhi = over_tok(lambda t: ((t // m) ^ 2) * m + t % m)
    to_core = over_tp(lambda t: t ^ 1)
    to_x = over_tp(lambda t: t ^ 2)

    def within_quad(a, by):
        pairs = [(t, t + by) for t in range(n) if 0 <= t + by < n and t // QUAD == (t + by) // QUAD]
        return lax.ppermute(a, "tok", pairs)

    def place_of(dz, dy):
        return ((z ^ dz) * m) + (y - dy) % m

    gains = jnp.stack([gain_attn_in, gain_attn_out, gain_ffn_in, gain_ffn_out])
    gains_all = lax.all_gather(gains, "tok", axis=1, tiled=True).astype(f32)
    gain_one, gain_two, gain_three, gain_four = (gains_all[i] for i in range(4))

    attn_own = jnp.concatenate([w_query, w_key, w_value, w_out], axis=1)
    attn_z = [attn_own] + [z_shift(attn_own, k) for k in range(1, 4)]
    attn_buf = jnp.zeros((n,) + attn_own.shape, bf16)
    for k in range(4):
        zs = (z - k) % 4
        attn_buf = put(attn_buf, attn_z[k], zs * m + y)
        for j in range(1, m):
            attn_buf = put(attn_buf, y_shift(attn_z[k], j), zs * m + (y - j) % m)
    attn_mat = attn_buf.reshape(width, -1)
    qkv_cols = head_cols + 2 * kv_cols
    qkv_mat = attn_mat[:, :qkv_cols]
    out_mat = attn_mat[:, qkv_cols:]

    def halves(a, index):
        return lax.dynamic_slice_in_dim(a, index * half, half, 1)

    gu_keep = jnp.concatenate([halves(w_gate, zlo), halves(w_up, zlo)], axis=1)
    gu_send = jnp.concatenate([halves(w_gate, 1 - zlo), halves(w_up, 1 - zlo)], axis=1)
    d_keep, d_send = halves(w_down, zlo), halves(w_down, 1 - zlo)
    gu_keep, gu_send, d_keep, d_send, attn_z = lax.optimization_barrier(
        (gu_keep, gu_send, d_keep, d_send, attn_z)
    )

    def ffn_gather(keep, send):
        buffer = jnp.zeros((n,) + keep.shape, bf16)
        for r, block in ((0, keep), (1, to_zlo(send))):
            for h in range(2):
                piece = block if h == 0 else to_zhi(block)
                buffer = put(buffer, piece, place_of(r + 2 * h, 0))
                for j in range(1, m):
                    buffer = put(buffer, y_shift(piece, j), place_of(r + 2 * h, j))
        return buffer.reshape(width, -1)

    gu_mat = ffn_gather(gu_keep, gu_send)
    down_mat = ffn_gather(d_keep, d_send)

    def own_slice(a):
        return lax.dynamic_slice_in_dim(a, tpi * part, part, 0)

    def gather_tp(a):
        buffer = jnp.zeros((4,) + a.shape, a.dtype)
        other = to_x(a)
        pair = to_core(jnp.stack([a, other]))
        for k, block in enumerate((a, pair[0], other, pair[1])):
            buffer = put(buffer, block, tpi ^ k)
        return buffer.reshape((-1,) + a.shape[1:])

    def gather_pair(a):
        a_z = to_zlo(a)
        a_x = to_x(a)
        a_xz = to_x(a_z)
        side = jnp.concatenate([a, a_z, a_x, a_xz])
        return jnp.concatenate([side, to_core(side)])

    def reduce_pair(compute):
        far = compute(1).astype(bf16)
        near = compute(0) + to_core(far).astype(f32)
        near = near.reshape(2, 2, part, width)
        z_part = near[0, 1] + to_x(near[1, 1].astype(bf16)).astype(f32)
        own = near[0, 0] + to_x(near[1, 0].astype(bf16)).astype(f32)
        return own + to_zlo(z_part.astype(bf16)).astype(f32)

    def reduce_tp(compute):
        far = compute(1 - core).astype(bf16)
        near = compute(core) + to_core(far).astype(f32)
        near = near.reshape(2, part, width)
        return pick(near, x) + to_x(pick(near, 1 - x).astype(bf16)).astype(f32)

    def core_rows(a, c):
        return pick(a.reshape(2, 2, part, a.shape[1]), c, 1).reshape(2 * part, a.shape[1])

    own_index = tok * rows + jnp.arange(rows, dtype=jnp.int32)
    key_index = (tok - REACH) * rows + jnp.arange((REACH + 1) * rows, dtype=jnp.int32)
    seg_query, pos_query = token_places(seq_lengths, own_index)
    seg_key, pos_key = token_places(seq_lengths, key_index)
    allowed = (seg_query[:, None] == seg_key[None, :]) & (pos_key[None, :] <= pos_query[:, None])
    cosine, sine_tab = rope_tables(pos_query)
    score_scale = HEAD_DIM ** (-0.5)

    unit_one_all, _ = norm_parts(inputs.astype(f32))
    hidden_one = (unit_one_all * gain_one).astype(bf16)
    qkv = jnp.dot(hidden_one, qkv_mat, preferred_element_type=f32)
    qk_rot = rotate(
        qkv[:, : head_cols + kv_cols].reshape(rows, -1, HEAD_DIM), cosine, sine_tab
    ).astype(bf16)
    query_rot = qk_rot[:, :heads]
    key_value = jnp.concatenate(
        [qk_rot[:, heads:].reshape(rows, kv_cols), qkv[:, head_cols + kv_cols :].astype(bf16)], axis=1
    )
    window = [within_quad(key_value, by) for by in range(REACH, 0, -1)] + [key_value]
    window = jnp.concatenate(window, axis=0)
    key_win, value_win = window[:, :kv_cols], window[:, kv_cols:]

    def capped_scores():
        raw = jnp.einsum("qjd,kd->jqk", query_rot, key_win, preferred_element_type=f32)
        capped = softcap_limit * jnp.tanh(raw * score_scale / softcap_limit)
        return (capped, jnp.where(allowed[None], capped, negative_fill))

    capped_fwd, masked_fwd = capped_scores()
    row_max = jnp.max(masked_fwd, axis=-1, keepdims=True)
    exponent = jnp.exp(masked_fwd - row_max)
    row_total = jnp.sum(exponent, axis=-1, keepdims=True)
    log_total = row_max + jnp.log(row_total)
    probs_low = (exponent / row_total).astype(bf16)
    attended = (
        jnp.einsum("jqk,kd->qjd", probs_low, value_win, preferred_element_type=f32)
        .reshape(rows, head_cols)
        .astype(bf16)
    )
    attn = reduce_tp(lambda c: contract_cols(core_rows(attended, c), out_mat))

    resid = own_slice(inputs).astype(f32)
    unit_two, inv_two = norm_parts(attn)
    resid_mid = resid + unit_two * gain_two
    unit_three, inv_three = norm_parts(resid_mid)
    hidden_two = gather_pair((unit_three * gain_three).astype(bf16))
    gate_up = jnp.dot(hidden_two, gu_mat, preferred_element_type=f32)
    gate_vals, up_vals = gate_up[:, :half], gate_up[:, half:]
    activated, gelu_pull = jax.vjp(partial(jax.nn.gelu, approximate=True), gate_vals)
    inner = (activated * up_vals).astype(bf16)
    ffn = reduce_pair(lambda k: contract_cols(jnp.split(inner, 2)[k], down_mat))
    unit_four, inv_four = norm_parts(ffn)
    layer_out = gather_tp((resid_mid + unit_four * gain_four).astype(bf16))

    grad_out = own_slice(out_grad).astype(f32)
    d_ffn, grad_four = norm_back(grad_out, gain_four, unit_four, inv_four)
    d_ffn_all = gather_pair(d_ffn.astype(bf16))
    d_inner = jnp.dot(d_ffn_all, down_mat, preferred_element_type=f32)

    def scatter_y(grad):
        blocks = grad.reshape(4, m, wrows, -1)
        total = pick(blocks, y, 1).astype(f32)
        for j in range(1, m):
            total = total + y_shift(pick(blocks, (y + j) % m, 1), j).astype(f32)
        return total

    def ffn_scatter(grad):
        total = scatter_y(grad.astype(bf16)).reshape(2, 2, wrows, -1)
        total = pick(total, zhi) + to_zhi(pick(total, 1 - zhi).astype(bf16)).astype(f32)
        return pick(total, zlo), to_zlo(pick(total, 1 - zlo).astype(bf16)).astype(f32)

    def sides(own, other):
        return jnp.where(
            zlo == 0,
            jnp.concatenate([own, other], axis=1),
            jnp.concatenate([other, own], axis=1),
        )

    out_down = sides(*ffn_scatter(contract_rows(d_ffn_all, inner)))
    grad_upvals = (d_inner * activated).astype(bf16)
    grad_gatevals = gelu_pull(d_inner * up_vals)[0].astype(bf16)
    grad_gu = jnp.concatenate([grad_gatevals, grad_upvals], axis=1)
    d_hidden_two = reduce_pair(lambda k: contract_cols(jnp.split(grad_gu, 2)[k], gu_mat))
    gu_own, gu_other = ffn_scatter(contract_rows(hidden_two, grad_gu))
    out_gate = sides(gu_own[:, :half], gu_other[:, :half])
    out_up = sides(gu_own[:, half:], gu_other[:, half:])

    mid_add, grad_three = norm_back(d_hidden_two, gain_three, unit_three, inv_three)
    d_mid = grad_out + mid_add

    d_attn, grad_two = norm_back(d_mid, gain_two, unit_two, inv_two)
    d_attn_low = gather_tp(d_attn.astype(bf16))

    def attn_scatter(grad):
        total = scatter_y(grad.astype(bf16))
        own = pick(total, z)
        for k in range(1, 4):
            own = own + z_shift(pick(total, (z + k) % 4).astype(bf16), k).astype(f32)
        return own

    out_wout = attn_scatter(contract_rows(d_attn_low, attended))
    d_attended = jnp.dot(d_attn_low, out_mat, preferred_element_type=f32).astype(bf16)
    d_att = d_attended.reshape(rows, heads, HEAD_DIM)
    capped_bwd, masked_bwd = capped_scores()
    probs = jnp.exp(masked_bwd - log_total)
    d_probs = jnp.einsum("qjd,kd->jqk", d_att, value_win, preferred_element_type=f32)
    d_value_win = jnp.einsum("jqk,qjd->kd", probs.astype(bf16), d_att, preferred_element_type=f32)
    row_delta = jnp.sum(probs * d_probs, axis=-1, keepdims=True)
    ratio_cap = capped_bwd / softcap_limit
    d_raw = (probs * (d_probs - row_delta) * (1.0 - ratio_cap * ratio_cap) * score_scale).astype(
        bf16
    )
    d_query_rot = jnp.einsum("jqk,kd->qjd", d_raw, key_win, preferred_element_type=f32)
    d_key_win = jnp.einsum("jqk,qjd->kd", d_raw, query_rot, preferred_element_type=f32)
    d_window = jnp.concatenate([d_key_win, d_value_win], axis=1).reshape(REACH + 1, rows, -1)
    d_kv = d_window[REACH]
    for by in range(1, REACH + 1):
        d_kv = d_kv + within_quad(d_window[REACH - by].astype(bf16), -by).astype(f32)
    d_query = rotate(d_query_rot, cosine, -sine_tab).reshape(rows, head_cols)
    d_key = rotate(d_kv[:, :kv_cols].reshape(rows, -1, HEAD_DIM), cosine, -sine_tab).reshape(
        rows, kv_cols
    )
    d_qkv = jnp.concatenate([d_query, d_key, d_kv[:, kv_cols:]], axis=1).astype(bf16)
    out_qkv = attn_scatter(contract_rows(hidden_one, d_qkv))
    d_hidden_one = reduce_tp(lambda c: contract_cols(core_rows(d_qkv, c), qkv_mat))
    unit_one, inv_one = norm_parts(resid)
    input_add, grad_one = norm_back(d_hidden_one, gain_one, unit_one, inv_one)
    input_grad = gather_tp(d_mid + input_add)

    gain_grads = lax.psum(jnp.stack([grad_one, grad_two, grad_three, grad_four]), ("tok", "tp"))
    gain_grads = lax.dynamic_slice_in_dim(gain_grads, tok * wrows, wrows, 1)
    return (
        layer_out,
        input_grad,
        gain_grads[0],
        gain_grads[1],
        gain_grads[2],
        gain_grads[3],
        out_qkv[:, :head_cols],
        out_qkv[:, head_cols : head_cols + kv_cols],
        out_qkv[:, head_cols + kv_cols :],
        out_wout,
        out_gate,
        out_up,
        out_down,
    )


def solution(mesh):
    weight = P("tok", "tp")
    in_specs = (P("tok", None), P()) + (P("tok"),) * 4 + (weight,) * 7 + (P("tok", None),)
    out_specs = (P("tok", None),) * 2 + (P("tok"),) * 4 + (weight,) * 7
    return jax.shard_map(local, mesh=mesh, in_specs=in_specs, out_specs=out_specs, check_vma=False)
```

```python
from functools import partial

import jax
import jax.numpy as jnp
from jax import lax
from jax.experimental import pallas as pl
from jax.experimental.pallas import tpu as pltpu
from jax.sharding import PartitionSpec as P

HEAD_DIM = 256
QUAD = 4
REACH = 2

softcap_limit = 50.0
norm_epsilon = 1e-06
rope_base = 10000.0
negative_fill = -1e30

QKV_COST = 10_000_000_000
ATTEND_COST = 20_000_000_000
ATTEND_BACK_COST = 40_000_000_000

f32 = jnp.float32
bf16 = jnp.bfloat16


def norm_parts(values):
    inverse = lax.rsqrt(jnp.mean(values * values, axis=-1, keepdims=True) + norm_epsilon)
    return values * inverse, inverse


def norm_back(gradient, gain_vec, unit_vals, inverse):
    scaled = gradient * gain_vec
    input_part = inverse * (
        scaled - unit_vals * jnp.mean(scaled * unit_vals, axis=-1, keepdims=True)
    )
    return (input_part, jnp.sum(gradient * unit_vals, axis=0))


def sequence_start(seq_lengths, tok_index):
    count = seq_lengths.shape[0]
    before = jnp.arange(count)[:, None] > jnp.arange(count)[None, :]
    starts = jnp.sum(jnp.where(before, seq_lengths[None, :], 0), axis=1)
    passed = tok_index[:, None] >= starts[None, :]
    return jnp.max(jnp.where(passed, starts[None, :], 0), axis=1)


def rope_tables(position):
    half_dim = HEAD_DIM // 2
    freqs = rope_base ** (-2.0 * jnp.arange(half_dim).astype(f32) / HEAD_DIM)
    theta = position.astype(f32)[:, None] * freqs[None, :]
    return (jnp.cos(theta), jnp.sin(theta))


def contract_rows(left, right):
    return lax.dot_general(
        left, right, (((0,), (0,)), ((), ())), preferred_element_type=f32
    )


def contract_cols(left, right):
    return lax.dot_general(
        left, right, (((1,), (1,)), ((), ())), preferred_element_type=f32
    )


def rotate_in(values, cosine, sine_tab):
    half_dim = HEAD_DIM // 2
    front, back = values[:, :half_dim], values[:, half_dim:]
    return jnp.concatenate(
        [front * cosine - back * sine_tab, back * cosine + front * sine_tab], axis=1
    )


def qkv_kernel(heads, kv_heads, x_ref, gain_ref, w_ref, cos_ref, sin_ref, hidden_ref, q_ref, kv_ref):
    which = pl.program_id(0)

    @pl.when(which == 0)
    def _():
        values = x_ref[...].astype(f32)
        inverse = lax.rsqrt(jnp.mean(values * values, axis=1, keepdims=True) + norm_epsilon)
        hidden_ref[...] = (values * inverse * gain_ref[...]).astype(bf16)

    product = jnp.dot(
        hidden_ref[...], w_ref[...], preferred_element_type=f32
    )

    @pl.when(which < heads)
    def _():
        q_ref[...] = rotate_in(product, cos_ref[...], sin_ref[...]).astype(bf16)

    @pl.when((which >= heads) & (which < heads + kv_heads))
    def _():
        kv_ref[...] = rotate_in(product, cos_ref[...], sin_ref[...]).astype(bf16)

    @pl.when(which >= heads + kv_heads)
    def _():
        kv_ref[...] = product.astype(bf16)


def qkv_call(inputs, gain, mat, cosine, sine_tab, heads, kv_heads):
    rows, width = inputs.shape
    whole = lambda a: pl.BlockSpec(a.shape, lambda j: (0, 0))
    return pl.pallas_call(
        partial(qkv_kernel, heads, kv_heads),
        grid=(heads + 2 * kv_heads,),
        out_shape=(
            jax.ShapeDtypeStruct((rows, width), bf16),
            jax.ShapeDtypeStruct((rows, heads * HEAD_DIM), bf16),
            jax.ShapeDtypeStruct((rows, 2 * kv_heads * HEAD_DIM), bf16),
        ),
        in_specs=[
            whole(inputs),
            whole(gain),
            pl.BlockSpec((width, HEAD_DIM), lambda j: (0, j)),
            whole(cosine),
            whole(sine_tab),
        ],
        out_specs=(
            pl.BlockSpec((rows, width), lambda j: (0, 0)),
            pl.BlockSpec((rows, HEAD_DIM), lambda j: (0, jnp.minimum(j, heads - 1))),
            pl.BlockSpec((rows, HEAD_DIM), lambda j: (0, jnp.maximum(j - heads, 0))),
        ),
        compiler_params=pltpu.CompilerParams(vmem_limit_bytes=40 << 20),
        cost_estimate=pl.CostEstimate(flops=QKV_COST, bytes_accessed=0, transcendentals=0),
        name="qkv",
    )(inputs, gain, mat, cosine, sine_tab)


def scores_of(q, k_refs, low, first_row, kv_heads, head):
    rows, block = q.shape[0], k_refs[0].shape[0]
    last = len(k_refs) - 1
    query_at = last * block + first_row + lax.broadcasted_iota(jnp.int32, (rows, 1), 0)
    found = []
    for i, ref in enumerate(k_refs):
        raw = lax.dot_general(
            q, ref[...], (((1,), (1,)), ((), ())), preferred_element_type=f32
        )
        ratio = jnp.tanh(raw * (HEAD_DIM ** (-0.5) / softcap_limit))
        key_at = i * block + lax.broadcasted_iota(jnp.int32, (1, block), 1)
        found.append((ratio, (key_at >= low) & (key_at <= query_at)))
    return found


def attend_kernel(tile, q_ref, k2_ref, k1_ref, k0_ref, v2_ref, v1_ref, v0_ref, low_ref, o_ref, lse_ref):
    step = pl.program_id(1)
    k_refs, v_refs = (k2_ref, k1_ref, k0_ref), (v2_ref, v1_ref, v0_ref)
    found = scores_of(q_ref[...], k_refs, low_ref[...], step * tile, 1, 0)
    masked = [jnp.where(ok, softcap_limit * ratio, negative_fill) for ratio, ok in found]
    row_max = jnp.max(masked[0], axis=1, keepdims=True)
    for part in masked[1:]:
        row_max = jnp.maximum(row_max, jnp.max(part, axis=1, keepdims=True))
    exps = [jnp.exp(part - row_max) for part in masked]
    total = sum(jnp.sum(e, axis=1, keepdims=True) for e in exps)
    scale = 1.0 / total
    mixed = sum(
        jnp.dot((e * scale).astype(bf16), v[...], preferred_element_type=f32)
        for e, v in zip(exps, v_refs)
    )
    o_ref[...] = mixed.astype(bf16)
    lse_ref[0] = row_max + jnp.log(total)


def attend_call(query, window, low, heads, kv_heads):
    rows = query.shape[0]
    tile = rows // 3
    group = heads // kv_heads
    key = pl.BlockSpec((rows, HEAD_DIM), lambda h, i: (0, h // group))
    value = pl.BlockSpec((rows, HEAD_DIM), lambda h, i: (0, kv_heads + h // group))
    mine = pl.BlockSpec((tile, HEAD_DIM), lambda h, i: (i, h))
    return pl.pallas_call(
        partial(attend_kernel, tile),
        grid=(heads, rows // tile),
        out_shape=(
            jax.ShapeDtypeStruct(query.shape, bf16),
            jax.ShapeDtypeStruct((heads, rows, 1), f32),
        ),
        in_specs=[mine] + [key] * 3 + [value] * 3 + [pl.BlockSpec((tile, 1), lambda h, i: (i, 0))],
        out_specs=(mine, pl.BlockSpec((1, tile, 1), lambda h, i: (h, i, 0))),
        compiler_params=pltpu.CompilerParams(vmem_limit_bytes=48 << 20),
        cost_estimate=pl.CostEstimate(flops=ATTEND_COST, bytes_accessed=0, transcendentals=0),
        name="attend",
    )(query, *window, *window, low)


def attend_back_kernel(
    tile, q_ref, do_ref, k2_ref, k1_ref, k0_ref, v2_ref, v1_ref, v0_ref, low_ref, lse_ref, cos_ref, sin_ref,
    dq_ref, d2_ref, d1_ref, d0_ref, acc_ref,
):
    head, step = pl.program_id(0), pl.program_id(1)
    k_refs, v_refs = (k2_ref, k1_ref, k0_ref), (v2_ref, v1_ref, v0_ref)

    @pl.when((head == 0) & (step == 0))
    def _():
        acc_ref[...] = jnp.zeros_like(acc_ref)

    q, d_out = q_ref[...], do_ref[...]
    found = scores_of(q, k_refs, low_ref[...], step * tile, 1, 0)
    lse = lse_ref[0]
    probs = [jnp.where(ok, jnp.exp(softcap_limit * ratio - lse), 0.0) for ratio, ok in found]
    d_probs = [
        lax.dot_general(d_out, v[...], (((1,), (1,)), ((), ())), preferred_element_type=f32)
        for v in v_refs
    ]
    delta = sum(jnp.sum(p * d, axis=1, keepdims=True) for p, d in zip(probs, d_probs))
    d_query = 0.0
    for i, (p, d) in enumerate(zip(probs, d_probs)):
        ratio = found[i][0]
        d_raw = (p * (d - delta) * (1.0 - ratio * ratio) * (HEAD_DIM ** (-0.5))).astype(bf16)
        d_query += jnp.dot(d_raw, k_refs[i][...], preferred_element_type=f32)
        acc_ref[i, :, :HEAD_DIM] += contract_rows(d_raw, q)
        acc_ref[i, :, HEAD_DIM:] += contract_rows(p.astype(bf16), d_out)
    dq_ref[...] = rotate_in(d_query, cos_ref[...], -sin_ref[...]).astype(bf16)

    @pl.when((head == pl.num_programs(0) - 1) & (step == pl.num_programs(1) - 1))
    def _():
        d2_ref[...] = acc_ref[0].astype(bf16)
        d1_ref[...] = acc_ref[1].astype(bf16)
        d0_ref[...] = acc_ref[2]


def attend_back_call(query, d_out, window, low, lse, cosine, sine_tab, heads):
    rows = query.shape[0]
    tile = rows // 3
    key = pl.BlockSpec((rows, HEAD_DIM), lambda h, i: (0, 0))
    value = pl.BlockSpec((rows, HEAD_DIM), lambda h, i: (0, 1))
    mine = pl.BlockSpec((tile, HEAD_DIM), lambda h, i: (i, h))
    tab = pl.BlockSpec((tile, HEAD_DIM // 2), lambda h, i: (i, 0))
    back = pl.BlockSpec((rows, 2 * HEAD_DIM), lambda h, i: (0, 0))
    return pl.pallas_call(
        partial(attend_back_kernel, tile),
        grid=(heads, rows // tile),
        out_shape=(
            jax.ShapeDtypeStruct(query.shape, bf16),
            jax.ShapeDtypeStruct((rows, 2 * HEAD_DIM), bf16),
            jax.ShapeDtypeStruct((rows, 2 * HEAD_DIM), bf16),
            jax.ShapeDtypeStruct((rows, 2 * HEAD_DIM), f32),
        ),
        in_specs=[mine, mine]
        + [key] * 3
        + [value] * 3
        + [
            pl.BlockSpec((tile, 1), lambda h, i: (i, 0)),
            pl.BlockSpec((1, tile, 1), lambda h, i: (h, i, 0)),
            tab,
            tab,
        ],
        out_specs=(mine, back, back, back),
        scratch_shapes=[pltpu.VMEM((3, rows, 2 * HEAD_DIM), f32)],
        compiler_params=pltpu.CompilerParams(vmem_limit_bytes=56 << 20),
        cost_estimate=pl.CostEstimate(flops=ATTEND_BACK_COST, bytes_accessed=0, transcendentals=0),
        name="attend_back",
    )(query, d_out, *window, *window, low, lse, cosine, sine_tab)


def pick(array, index, axis=0):
    return lax.dynamic_index_in_dim(array, index, axis, keepdims=False)


class Order:
    def __init__(self, token):
        self.token = token

    def __call__(self, *values):
        values, self.token = lax.optimization_barrier((values, self.token))
        return values[0] if len(values) == 1 else values


def put(buffer, block, index):
    return lax.dynamic_update_index_in_dim(buffer, block, index, 0)


def local(
    inputs,
    seq_lengths,
    gain_attn_in,
    gain_attn_out,
    gain_ffn_in,
    gain_ffn_out,
    w_query,
    w_key,
    w_value,
    w_out,
    w_gate,
    w_up,
    w_down,
    out_grad,
):
    n = lax.axis_size("tok")
    m = n // 4
    width = inputs.shape[1]
    rows = inputs.shape[0]
    part = rows // 4
    tok = lax.axis_index("tok")
    tpi = lax.axis_index("tp")
    z, y = tok // m, tok % m
    zlo, zhi = z % 2, z // 2
    x, core = tpi // 2, tpi % 2
    wrows = w_query.shape[0]
    head_cols = w_query.shape[1]
    kv_cols = w_key.shape[1]
    heads = head_cols // HEAD_DIM
    kv_heads = kv_cols // HEAD_DIM
    units = w_gate.shape[1]
    half = units // 2

    def over_tok(fn):
        pairs = [(t, fn(t)) for t in range(n)]
        return lambda a: lax.ppermute(a, "tok", pairs)

    def over_tp(fn):
        pairs = [(t, fn(t)) for t in range(4)]
        return lambda a: lax.ppermute(a, "tp", pairs)

    def z_shift(a, k):
        return over_tok(lambda t: ((t // m + k) % 4) * m + t % m)(a)

    def y_shift(a, k):
        return over_tok(lambda t: (t // m) * m + (t % m + k) % m)(a)

    to_zlo = over_tok(lambda t: ((t // m) ^ 1) * m + t % m)
    to_zhi = over_tok(lambda t: ((t // m) ^ 2) * m + t % m)
    to_core = over_tp(lambda t: t ^ 1)
    to_x = over_tp(lambda t: t ^ 2)

    def within_quad(a, by):
        pairs = [(t, t + by) for t in range(n) if 0 <= t + by < n and t // QUAD == (t + by) // QUAD]
        return lax.ppermute(a, "tok", pairs)

    def place_of(dz, dy):
        return ((z ^ dz) * m) + (y - dy) % m

    step = Order(seq_lengths)

    def z_line(a, way, at):
        pairs = [
            (zs * m + ys, (zs + way) * m + ys)
            for zs in (range(at - 1, 3) if way > 0 else range(1, 5 - at))
            for ys in range(m)
        ]
        return lax.ppermute(a, "tok", pairs)

    def y_others(a):
        return [y_shift(a, j) for j in range(1, m)]

    def halves(a, index):
        return lax.dynamic_slice_in_dim(a, index * half, half, 1)

    attn_own = jnp.concatenate([w_query, w_key, w_value, w_out], axis=1)
    gains = jnp.concatenate([gain_attn_in, gain_attn_out, gain_ffn_in, gain_ffn_out])
    attn_cols = attn_own.shape[1]
    gains = jnp.pad(gains, (0, attn_cols - gains.shape[0])).reshape(1, attn_cols)
    attn_own = jnp.concatenate([attn_own, jnp.pad(gains, ((0, 7), (0, 0)))], axis=0)
    up1, down1 = z_line(attn_own, 1, 1), z_line(attn_own, -1, 1)
    attn_y = {0: y_others(attn_own)}
    gu_keep = jnp.concatenate([halves(w_gate, zlo), halves(w_up, zlo)], axis=1)
    gu_send = jnp.concatenate([halves(w_gate, 1 - zlo), halves(w_up, 1 - zlo)], axis=1)
    d_keep, d_send = halves(w_down, zlo), halves(w_down, 1 - zlo)
    gu_y = {0: y_others(gu_keep)}
    up1, down1 = step(up1, down1)
    up2, down2 = z_line(up1, 1, 2), z_line(down1, -1, 2)
    up2, down2 = step(up2, down2)
    attn_z = {0: attn_own, 2: jnp.where(z >= 2, up2, down2)}
    up3, down3 = z_line(up2, 1, 3), z_line(down2, -1, 3)
    attn_y[2] = y_others(attn_z[2])
    gu_send, gu_first, d_send = step(gu_send, gu_keep, d_send)
    gu_z = {0: gu_keep, 1: to_zlo(gu_send)}
    gu_z[2] = to_zhi(gu_first)
    d_z = {0: d_keep, 1: to_zlo(d_send)}
    up3, down3 = step(up3, down3)
    attn_z[1] = jnp.where(z >= 1, up1, down3)
    attn_z[3] = jnp.where(z >= 3, up3, down1)
    attn_y[1], attn_y[3] = y_others(attn_z[1]), y_others(attn_z[3])
    gu_z[1] = step(gu_z[1])
    gu_y[1] = y_others(gu_z[1])
    gu_z[3] = to_zhi(gu_z[1])
    attn_y = step(attn_y)

    attn_buf = jnp.zeros((n,) + attn_own.shape, bf16)
    for k in range(4):
        for j, piece in enumerate([attn_z[k]] + attn_y[k]):
            attn_buf = put(attn_buf, piece, ((z - k) % 4) * m + (y - j) % m)
    gains_all = attn_buf[:, wrows, : 4 * wrows].reshape(n, 4, wrows)
    gains_all = gains_all.transpose(1, 0, 2).reshape(4, 1, width).astype(f32)
    gain_one, gain_two, gain_three, gain_four = (gains_all[i] for i in range(4))

    def ffn_matrix(by_z, by_y):
        buffer = jnp.zeros((n,) + by_z[0].shape, bf16)
        for k in range(4):
            for j, piece in enumerate([by_z[k]] + by_y[k]):
                buffer = put(buffer, piece, (z ^ k) * m + (y - j) % m)
        return buffer.reshape(width, -1)

    def own_slice(a):
        return lax.dynamic_slice_in_dim(a, tpi * part, part, 0)

    def gather_tp(a):
        buffer = jnp.zeros((4,) + a.shape, a.dtype)
        low = a.astype(bf16)
        other = to_x(low)
        pair = to_core(jnp.stack([low, other]))
        for k, block in enumerate((a, pair[0], other, pair[1])):
            buffer = put(buffer, block.astype(a.dtype), tpi ^ k)
        return buffer.reshape((-1,) + a.shape[1:])

    def gather_pair(a):
        a_z = to_zlo(a)
        a_x = to_x(a)
        mid = width // 2
        a_xz = jnp.concatenate([to_x(a_z[:, :mid]), to_zlo(a_x[:, mid:])], axis=1)
        side = jnp.concatenate([a, a_z, a_x, a_xz])
        return jnp.concatenate([side, to_core(side)])

    def reduce_pair(compute):
        far = compute(1).astype(bf16)
        near = compute(0) + to_core(far).astype(f32)
        near = near.reshape(2, 2, part, width)
        mid = width // 2
        left, right = near[..., :mid], near[..., mid:]
        left = left[0] + to_x(left[1].astype(bf16)).astype(f32)
        right = right[:, 0] + to_zlo(right[:, 1].astype(bf16)).astype(f32)
        left = left[0] + to_zlo(left[1].astype(bf16)).astype(f32)
        right = right[0] + to_x(right[1].astype(bf16)).astype(f32)
        return jnp.concatenate([left, right], axis=1)

    def reduce_tp(compute):
        far = compute(1 - core).astype(bf16)
        near = compute(core) + to_core(far).astype(f32)
        near = near.reshape(2, part, width)
        return pick(near, x) + to_x(pick(near, 1 - x).astype(bf16)).astype(f32)

    def core_rows(a, c):
        return pick(a.reshape(2, 2, part, a.shape[1]), c, 1).reshape(2 * part, a.shape[1])

    own_index = tok * rows + jnp.arange(rows, dtype=jnp.int32)
    seq_start = sequence_start(seq_lengths, own_index)
    cosine, sine_tab = rope_tables(own_index - seq_start)
    low = (seq_start - (tok - REACH) * rows)[:, None]

    qkv_cols = head_cols + 2 * kv_cols
    qkv_mat = attn_buf[:, :wrows, :qkv_cols].reshape(width, qkv_cols)
    out_mat = attn_buf[:, :wrows, qkv_cols:].reshape(width, head_cols)
    hidden_one, query, key_value = qkv_call(
        inputs, gain_one, qkv_mat, cosine, sine_tab, heads, kv_heads
    )
    key_value = step(key_value)
    window = [within_quad(key_value, by) for by in range(REACH, 0, -1)] + [key_value]
    gu_z[2], d_z[1], d_first = step(gu_z[2], d_z[1], d_keep)
    gu_y[2] = y_others(gu_z[2])
    d_y = {0: y_others(d_first), 1: y_others(d_z[1])}
    d_z[2], d_z[3] = to_zhi(d_first), to_zhi(d_z[1])
    window = step(window)
    attended, lse = attend_call(query, window, low, heads, kv_heads)
    attended = step(attended)
    attn = reduce_tp(lambda c: contract_cols(core_rows(attended, c), out_mat))
    gu_z[3] = step(gu_z[3])
    gu_y[3] = y_others(gu_z[3])
    d_z[2] = step(d_z[2])
    d_y[2] = y_others(d_z[2])
    attn, d_z[3] = step(attn, d_z[3])
    d_y[3] = y_others(d_z[3])

    resid = own_slice(inputs).astype(f32)
    unit_two, inv_two = norm_parts(attn)
    resid_mid = resid + unit_two * gain_two
    unit_three, inv_three = norm_parts(resid_mid)
    hidden_two = gather_pair((unit_three * gain_three).astype(bf16))
    gu_mat, down_mat = ffn_matrix(gu_z, gu_y), ffn_matrix(d_z, d_y)
    gate_up = jnp.dot(hidden_two, gu_mat, preferred_element_type=f32)
    gate_vals, up_vals = gate_up[:, :half], gate_up[:, half:]
    activated, gelu_pull = jax.vjp(partial(jax.nn.gelu, approximate=True), gate_vals)
    inner = (activated * up_vals).astype(bf16)
    ffn = reduce_pair(lambda k: contract_cols(jnp.split(inner, 2)[k], down_mat))
    unit_four, inv_four = norm_parts(ffn)
    layer_out = gather_tp((resid_mid + unit_four * gain_four).astype(bf16))

    grad_out = own_slice(out_grad).astype(f32)
    d_ffn, grad_four = norm_back(grad_out, gain_four, unit_four, inv_four)
    d_ffn_all = gather_pair(d_ffn.astype(bf16))
    d_inner = jnp.dot(d_ffn_all, down_mat, preferred_element_type=f32)

    def y_send(grad):
        blocks = grad.astype(bf16).reshape(4, m, wrows, -1)
        return [pick(blocks, y, 1)] + [y_shift(pick(blocks, (y + j) % m, 1), j) for j in range(1, m)]

    def add_up(terms):
        return sum(t.astype(f32) for t in terms)

    def zhi_send(terms):
        total = add_up(terms).reshape(2, 2, wrows, -1)
        return [pick(total, zhi), to_zhi(pick(total, 1 - zhi).astype(bf16))]

    def zlo_send(terms):
        total = add_up(terms)
        return pick(total, zlo), to_zlo(pick(total, 1 - zlo).astype(bf16)).astype(f32)

    def z_send(terms):
        total = add_up(terms)
        return [pick(total, z)] + [
            z_shift(pick(total, (z + k) % 4).astype(bf16), k) for k in range(1, 4)
        ]

    def sides(own, other):
        return jnp.where(
            zlo == 0,
            jnp.concatenate([own, other], axis=1),
            jnp.concatenate([other, own], axis=1),
        )

    down_s = y_send(contract_rows(d_ffn_all, inner))
    grad_upvals = (d_inner * activated).astype(bf16)
    grad_gatevals = gelu_pull(d_inner * up_vals)[0].astype(bf16)
    grad_gu = jnp.concatenate([grad_gatevals, grad_upvals], axis=1)
    far, near = (contract_cols(jnp.split(grad_gu, 2)[k], gu_mat) for k in (1, 0))
    near = near + to_core(far.astype(bf16)).astype(f32)
    near = near.reshape(2, 2, part, width)
    mid = width // 2
    left, right = near[..., :mid], near[..., mid:]
    left_in, right_in = to_x(left[1].astype(bf16)), to_zlo(right[:, 1].astype(bf16))
    gate_s = y_send(contract_rows(hidden_two, grad_gatevals))
    up_s = y_send(contract_rows(hidden_two, grad_upvals))
    left_in, right_in = step(left_in, right_in)
    left = left[0] + left_in.astype(f32)
    right = right[:, 0] + right_in.astype(f32)
    left_in, right_in = to_zlo(left[1].astype(bf16)), to_x(right[1].astype(bf16))
    down_s = step(down_s)
    left_in, right_in = step(left_in, right_in)
    d_hidden_two = jnp.concatenate(
        [left[0] + left_in.astype(f32), right[0] + right_in.astype(f32)], axis=1
    )
    down_s = zhi_send(down_s)

    mid_add, grad_three = norm_back(d_hidden_two, gain_three, unit_three, inv_three)
    d_mid = grad_out + mid_add

    d_attn, grad_two = norm_back(d_mid, gain_two, unit_two, inv_two)
    d_attn_low = gather_tp(d_attn.astype(bf16))

    d_attn_low = step(d_attn_low)
    wout_s = contract_rows(d_attn_low, attended)
    d_attended = jnp.dot(d_attn_low, out_mat, preferred_element_type=f32).astype(bf16)
    gate_s, down_s = step(gate_s, down_s)
    gate_s = zhi_send(gate_s)
    d_query, *d_window, d_kv = attend_back_call(
        query, d_attended, window, low, lse, cosine, sine_tab, heads
    )
    d_window = [within_quad(d_window[REACH - by], -by) for by in range(1, REACH + 1)]
    q_grad = contract_rows(hidden_one, d_query)
    up_s, wout_s = step(up_s, wout_s)
    up_s, wout_s = zhi_send(up_s), y_send(wout_s)
    out_down = sides(*zlo_send(down_s))
    d_window = step(d_window)
    q_s = y_send(q_grad)
    d_kv = d_kv + add_up(d_window)
    d_key = rotate_in(d_kv[:, :kv_cols], cosine, -sine_tab)
    d_key_value = jnp.concatenate([d_key.astype(bf16), d_kv[:, kv_cols:].astype(bf16)], axis=1)
    d_qkv = jnp.concatenate([d_query, d_key_value], axis=1)
    kv_s = y_send(contract_rows(hidden_one, d_key_value))
    d_hidden_one = reduce_tp(lambda c: contract_cols(core_rows(d_qkv, c), qkv_mat))
    unit_one, inv_one = norm_parts(resid)
    input_add, grad_one = norm_back(d_hidden_one, gain_one, unit_one, inv_one)
    gate_s = step(gate_s)
    out_gate = sides(*zlo_send(gate_s))
    wout_s = z_send(step(wout_s))
    up_s = step(up_s)
    out_up = sides(*zlo_send(up_s))
    q_s = z_send(step(q_s))
    kv_s = z_send(step(kv_s))
    out_wout, out_q, out_kv = add_up(wout_s), add_up(q_s), add_up(kv_s)
    input_grad = gather_tp(d_mid + input_add)

    gain_grads = jnp.stack([grad_one, grad_two, grad_three, grad_four])
    gain_grads = gain_grads + to_core(gain_grads)
    gain_grads = gain_grads + to_x(gain_grads)
    bit = 1
    while bit < n:
        gain_grads = gain_grads + over_tok(lambda t: t ^ bit)(gain_grads)
        bit *= 2
    gain_grads = lax.dynamic_slice_in_dim(gain_grads, tok * wrows, wrows, 1)
    return (
        layer_out,
        input_grad,
        gain_grads[0],
        gain_grads[1],
        gain_grads[2],
        gain_grads[3],
        out_q,
        out_kv[:, :kv_cols],
        out_kv[:, kv_cols:],
        out_wout,
        out_gate,
        out_up,
        out_down,
    )


def solution(mesh):
    weight = P("tok", "tp")
    in_specs = (P("tok", None), P()) + (P("tok"),) * 4 + (weight,) * 7 + (P("tok", None),)
    out_specs = (P("tok", None),) * 2 + (P("tok"),) * 4 + (weight,) * 7
    return jax.shard_map(local, mesh=mesh, in_specs=in_specs, out_specs=out_specs, check_vma=False)
```

```python
from functools import partial

import jax
import jax.numpy as jnp
from jax import lax
from jax.experimental import pallas as pl
from jax.experimental.pallas import tpu as pltpu
from jax.sharding import PartitionSpec as P

HEAD_DIM = 256
QUAD = 4
REACH = 2

softcap_limit = 50.0
norm_epsilon = 1e-06
rope_base = 10000.0
negative_fill = -1e30

QKV_COST = 10_000_000_000
ATTEND_COST = 20_000_000_000
ATTEND_BACK_COST = 40_000_000_000

f32 = jnp.float32
bf16 = jnp.bfloat16


def norm_parts(values):
    inverse = lax.rsqrt(jnp.mean(values * values, axis=-1, keepdims=True) + norm_epsilon)
    return values * inverse, inverse


def norm_back(gradient, gain_vec, unit_vals, inverse):
    scaled = gradient * gain_vec
    input_part = inverse * (
        scaled - unit_vals * jnp.mean(scaled * unit_vals, axis=-1, keepdims=True)
    )
    return (input_part, jnp.sum(gradient * unit_vals, axis=0))


def sequence_start(seq_lengths, tok_index):
    count = seq_lengths.shape[0]
    before = jnp.arange(count)[:, None] > jnp.arange(count)[None, :]
    starts = jnp.sum(jnp.where(before, seq_lengths[None, :], 0), axis=1)
    passed = tok_index[:, None] >= starts[None, :]
    return jnp.max(jnp.where(passed, starts[None, :], 0), axis=1)


def rope_tables(position):
    half_dim = HEAD_DIM // 2
    freqs = rope_base ** (-2.0 * jnp.arange(half_dim).astype(f32) / HEAD_DIM)
    theta = position.astype(f32)[:, None] * freqs[None, :]
    return (jnp.cos(theta), jnp.sin(theta))


def contract_rows(left, right):
    return lax.dot_general(
        left, right, (((0,), (0,)), ((), ())), preferred_element_type=f32
    )


def contract_cols(left, right):
    return lax.dot_general(
        left, right, (((1,), (1,)), ((), ())), preferred_element_type=f32
    )


def gather_kernel(
    m, attn_ref, guk_ref, gus_ref, dk_ref, ds_ref, attn_buf, gu_buf, d_buf, send_sem, recv_sem, own_sem
):
    tok, tp = lax.axis_index("tok"), lax.axis_index("tp")
    z, y = tok // m, tok % m
    flip1 = z + 1 - 2 * (z % 2)
    flip2 = (z + 2) % 4
    flip3 = 3 - z
    slot = lambda zs, ys: zs * m + ys
    others = range(1, m)
    used = iter(range(9 + 8 * (m - 1)))

    def hop(src, dst, number, target):
        return pltpu.make_async_remote_copy(
            src_ref=src,
            dst_ref=dst,
            send_sem=send_sem.at[number],
            recv_sem=recv_sem.at[number],
            device_id=(target, tp),
            device_id_type=pl.DeviceIdType.MESH,
        )

    barrier = pltpu.get_barrier_semaphore()
    peers = [slot(f, y) for f in (flip1, flip2, flip3)] + [slot(z, (y + j) % m) for j in others]
    for peer in peers:
        pl.semaphore_signal(barrier, inc=1, device_id=(peer, tp), device_id_type=pl.DeviceIdType.MESH)
    pl.semaphore_wait(barrier, len(peers))

    own = [
        pltpu.make_async_copy(src, dst.at[tok], own_sem.at[i])
        for i, (src, dst) in enumerate(((attn_ref, attn_buf), (guk_ref, gu_buf), (dk_ref, d_buf)))
    ]
    ups = [next(used) for _ in range(3)]
    downs = [next(used) for _ in range(3)]
    y_own = {j: next(used) for j in others}
    y_gu = {j: next(used) for j in others}
    y_up = {(s, j): next(used) for s in (1, 2, 3) for j in others}
    y_down = {(s, j): next(used) for s in (1, 2, 3) for j in others}
    n_gu1, n_d1, n_gu2 = next(used), next(used), next(used)

    def line(step, way):
        at = slot(z - way * (step - 1), y)
        src = attn_ref if step == 1 else attn_buf.at[at]
        return hop(src, attn_buf.at[at], (ups if way > 0 else downs)[step - 1], slot(z + way, y))

    def can_send(step, way):
        return (z >= step - 1) & (z <= 2) if way > 0 else (z <= 4 - step) & (z >= 1)

    def can_take(step, way):
        return z >= step if way > 0 else z <= 3 - step

    def taken(step, way):
        at = slot(z - way * step, y)
        return hop(attn_buf.at[at], attn_buf.at[at], (ups if way > 0 else downs)[step - 1], tok)

    def relay(step, way, j, back):
        at = slot(z - way * step, (y - j) % m if back else y)
        number = (y_up if way > 0 else y_down)[step, j]
        return hop(attn_buf.at[at], attn_buf.at[at], number, slot(z, (y + j) % m))

    y_own_hops = [hop(attn_ref, attn_buf.at[tok], y_own[j], slot(z, (y + j) % m)) for j in others]
    y_gu_hops = [hop(guk_ref, gu_buf.at[tok], y_gu[j], slot(z, (y + j) % m)) for j in others]
    z_hops = [
        hop(gus_ref, gu_buf.at[tok], n_gu1, slot(flip1, y)),
        hop(guk_ref, gu_buf.at[tok], n_gu2, slot(flip2, y)),
        hop(ds_ref, d_buf.at[tok], n_d1, slot(flip1, y)),
    ]

    for way in (1, -1):
        pl.when(can_send(1, way))(line(1, way).start)
    for c in y_own_hops + y_gu_hops + own:
        c.start()
    for step in (1, 2, 3):
        for way in (1, -1):

            @pl.when(can_take(step, way))
            def _(step=step, way=way):
                taken(step, way).wait_recv()
                if step < 3:
                    pl.when(can_send(step + 1, way))(line(step + 1, way).start)
                for j in others:
                    relay(step, way, j, False).start()

        if step == 2:
            for c in z_hops:
                c.start()
    for j in others:
        at = slot(z, (y - j) % m)
        hop(attn_buf.at[at], attn_buf.at[at], y_own[j], tok).wait_recv()
        hop(gu_buf.at[at], gu_buf.at[at], y_gu[j], tok).wait_recv()
    for step in (1, 2, 3):
        for way in (1, -1):

            @pl.when(can_take(step, way))
            def _(step=step, way=way):
                for j in others:
                    relay(step, way, j, True).wait_recv()
                    relay(step, way, j, False).wait_send()

            pl.when(can_send(step, way))(line(step, way).wait_send)
    for number, ref, f in ((n_gu1, gu_buf, flip1), (n_d1, d_buf, flip1), (n_gu2, gu_buf, flip2)):
        at = slot(f, y)
        hop(ref.at[at], ref.at[at], number, tok).wait_recv()
    for c in y_own_hops + y_gu_hops + z_hops:
        c.wait_send()
    for c in own:
        c.wait()


def gather_call(n, attn, gu_keep, gu_send, d_keep, d_send):
    m = n // 4
    count = 9 + 8 * (m - 1)
    hbm = pl.BlockSpec(memory_space=pltpu.HBM)
    return pl.pallas_call(
        partial(gather_kernel, m),
        out_shape=tuple(jax.ShapeDtypeStruct((n,) + a.shape, bf16) for a in (attn, gu_keep, d_keep)),
        in_specs=[hbm] * 5,
        out_specs=(hbm,) * 3,
        scratch_shapes=[
            pltpu.SemaphoreType.DMA((count,)),
            pltpu.SemaphoreType.DMA((count,)),
            pltpu.SemaphoreType.DMA((3,)),
        ],
        compiler_params=pltpu.CompilerParams(collective_id=0, has_side_effects=True),
        name="gather_first",
    )(attn, gu_keep, gu_send, d_keep, d_send)


def tie_kernel(*refs):
    del refs


def tie(values, *earlier):
    leaves, tree = jax.tree.flatten(values)
    earlier = jax.tree.leaves(earlier)
    anywhere = pl.BlockSpec(memory_space=pl.ANY)
    found = pl.pallas_call(
        tie_kernel,
        out_shape=tuple(jax.ShapeDtypeStruct(v.shape, v.dtype) for v in leaves),
        in_specs=[anywhere] * (len(leaves) + len(earlier)),
        out_specs=(anywhere,) * len(leaves),
        input_output_aliases={i: i for i in range(len(leaves))},
        name="tie",
    )(*leaves, *earlier)
    return jax.tree.unflatten(tree, found)


def add_rows(total_ref, arrived_ref):
    block = 32 if total_ref.shape[0] % 32 == 0 else total_ref.shape[0]

    def body(i, carry):
        at = pl.ds(pl.multiple_of(i * block, block), block)
        total_ref[at, :] = total_ref[at, :] + arrived_ref[at, :].astype(f32)
        return carry

    lax.fori_loop(0, total_ref.shape[0] // block, body, 0)


def round_rows(out_ref, value_ref):
    block = 32 if out_ref.shape[0] % 32 == 0 else out_ref.shape[0]

    def body(i, carry):
        at = pl.ds(pl.multiple_of(i * block, block), block)
        out_ref[at, :] = value_ref[at, :].astype(out_ref.dtype)
        return carry

    lax.fori_loop(0, out_ref.shape[0] // block, body, 0)


def comm_kernel(m, chain, kinds, *refs):
    count = {"gather_pair": 1, "gather_tp": 1, "reduce_pair": 2, "reduce_tp": 2}[chain]
    ins, refs = refs[:count], refs[count:]
    sent, refs = refs[: len(kinds)], refs[len(kinds) :]
    out_ref, refs = refs[0], refs[1:]
    landed, refs = refs[: len(kinds)], refs[len(kinds) :]
    send_sem, recv_sem, own_sem = refs[:3]
    scratch = refs[3:]
    tok, tp = lax.axis_index("tok"), lax.axis_index("tp")
    z, y = tok // m, tok % m
    x, c = tp // 2, tp % 2
    others = range(1, m)
    zlo = ((z + 1 - 2 * (z % 2)) * m + y, tp)
    zhi = (((z + 2) % 4) * m + y, tp)
    over_x, over_core = (tok, (tp + 2) % 4), (tok, tp + 1 - 2 * c)
    used = iter(range(8 + len(kinds)))

    def hop(src, dst, target):
        number = next(used)
        return pltpu.make_async_remote_copy(
            src_ref=src,
            dst_ref=dst,
            send_sem=send_sem.at[number],
            recv_sem=recv_sem.at[number],
            device_id=target,
            device_id_type=pl.DeviceIdType.MESH,
        )

    def target(kind):
        if kind[0] == "y":
            return (z * m + (y + kind[1]) % m, tp)
        return {"zlo": zlo, "zhi": zhi}[kind[0]]

    peers = [over_x, over_core]
    if chain in ("gather_pair", "reduce_pair") or ("zlo",) in kinds:
        peers.append(zlo)
    if ("zhi",) in kinds:
        peers.append(zhi)
    if any(kind[0] == "y" for kind in kinds):
        peers += [(z * m + (y + j) % m, tp) for j in others]
    barrier = pltpu.get_barrier_semaphore()
    for peer in peers:
        pl.semaphore_signal(barrier, inc=1, device_id=peer, device_id_type=pl.DeviceIdType.MESH)
    pl.semaphore_wait(barrier, len(peers))

    beside = [hop(a, b, target(kind)) for a, b, kind in zip(sent, landed, kinds)]
    waits = []

    def start_beside():
        for b in beside:
            b.start()

    if chain == "gather_tp":
        (a_ref,) = ins
        own = pltpu.make_async_copy(a_ref, out_ref.at[tp], own_sem)
        there = (tp + 2) % 4
        first = hop(a_ref, out_ref.at[tp], over_x)
        near = hop(a_ref, out_ref.at[tp], over_core)
        far = hop(out_ref.at[there], out_ref.at[there], over_core)
        first.start()
        start_beside()
        near.start()
        own.start()
        first.wait_recv()
        far.start()
        near.wait_recv()
        far.wait_recv()
        own.wait()
        waits = [first, near, far]
    elif chain == "gather_pair":
        (a_ref,) = ins
        half = a_ref.shape[0] // 2
        top, low = pl.ds(0, half), pl.ds(half, half)
        own = pltpu.make_async_copy(a_ref, out_ref.at[0], own_sem)
        first_z = hop(a_ref, out_ref.at[1], zlo)
        first_x = hop(a_ref, out_ref.at[2], over_x)
        next_x = hop(out_ref.at[1, top], out_ref.at[3, top], over_x)
        next_z = hop(out_ref.at[2, low], out_ref.at[3, low], zlo)
        core = [
            hop(a_ref if k == 0 else out_ref.at[k], out_ref.at[4 + k], over_core) for k in range(4)
        ]
        first_z.start()
        first_x.start()
        own.start()
        core[0].start()
        start_beside()
        first_z.wait_recv()
        next_x.start()
        core[1].start()
        first_x.wait_recv()
        next_z.start()
        core[2].start()
        next_x.wait_recv()
        next_z.wait_recv()
        core[3].start()
        for each in core:
            each.wait_recv()
        own.wait()
        waits = [first_z, first_x, next_x, next_z] + core
    elif chain == "reduce_tp":
        far_ref, near_ref = ins
        near, from_core, to_go, from_x = scratch
        part = out_ref.shape[0]
        own = pltpu.make_async_copy(near_ref, near, own_sem)
        core = hop(far_ref, from_core, over_core)
        over = hop(to_go, from_x, over_x)
        core.start()
        own.start()
        start_beside()
        own.wait()
        core.wait_recv()
        away = pl.ds(pl.multiple_of((1 - x) * part, part), part)
        here = pl.ds(pl.multiple_of(x * part, part), part)
        add_rows(near.at[away], from_core.at[away])
        round_rows(to_go, near.at[away])
        over.start()
        add_rows(near.at[here], from_core.at[here])
        round_rows(out_ref, near.at[here])
        over.wait_recv()
        add_rows(out_ref, from_x)
        waits = [core, over]
    else:
        far_ref, near_ref = ins
        near, from_core, left_go, left_in, right_go, right_in = scratch
        part, width = out_ref.shape
        mid = width // 2
        left, right = pl.ds(0, mid), pl.ds(mid, mid)
        rows = lambda k, count=1: pl.ds(k * part, count * part)
        own = pltpu.make_async_copy(near_ref, near, own_sem)
        core = hop(far_ref, from_core, over_core)
        left_x = hop(left_go.at[rows(0, 2)], left_in.at[rows(0, 2)], over_x)
        right_z = hop(right_go.at[rows(0, 2)], right_in.at[rows(0, 2)], zlo)
        left_z = hop(left_go.at[rows(2)], left_in.at[rows(2)], zlo)
        right_x = hop(right_go.at[rows(2)], right_in.at[rows(2)], over_x)
        core.start()
        own.start()
        start_beside()
        own.wait()
        core.wait_recv()
        add_rows(near.at[rows(1, 3)], from_core.at[rows(1, 3)])
        round_rows(left_go.at[rows(0, 2)], near.at[rows(2, 2), left])
        left_x.start()
        round_rows(right_go.at[rows(0)], near.at[rows(1), right])
        round_rows(right_go.at[rows(1)], near.at[rows(3), right])
        right_z.start()
        add_rows(near.at[rows(0)], from_core.at[rows(0)])
        left_x.wait_recv()
        add_rows(near.at[rows(0, 2), left], left_in.at[rows(0, 2)])
        round_rows(left_go.at[rows(2)], near.at[rows(1), left])
        left_z.start()
        right_z.wait_recv()
        add_rows(near.at[rows(0), right], right_in.at[rows(0)])
        add_rows(near.at[rows(2), right], right_in.at[rows(1)])
        round_rows(right_go.at[rows(2)], near.at[rows(2), right])
        right_x.start()
        round_rows(out_ref, near.at[rows(0)])
        left_z.wait_recv()
        add_rows(out_ref.at[:, left], left_in.at[rows(2)])
        right_x.wait_recv()
        add_rows(out_ref.at[:, right], right_in.at[rows(2)])
        waits = [core, left_x, right_z, left_z, right_x]
    for each in waits:
        each.wait_send()
    for b in beside:
        b.wait_recv()
        b.wait_send()


def comm_call(n, number, chain, ins, beside=()):
    m = n // 4
    kinds = tuple(kind for _, kind in beside)
    arrays = [a for a, _ in beside]
    hbm = pl.BlockSpec(memory_space=pltpu.HBM)
    vmem = pl.BlockSpec(memory_space=pltpu.VMEM)
    rows, width = ins[-1].shape
    scratch = []
    if chain == "gather_tp":
        out = jax.ShapeDtypeStruct((4, rows, width), bf16)
    elif chain == "gather_pair":
        out = jax.ShapeDtypeStruct((8, rows, width), bf16)
    elif chain == "reduce_tp":
        out = jax.ShapeDtypeStruct((rows // 2, width), f32)
        scratch = [
            pltpu.VMEM((rows, width), f32),
            pltpu.VMEM((rows, width), bf16),
            pltpu.VMEM((rows // 2, width), bf16),
            pltpu.VMEM((rows // 2, width), bf16),
        ]
    else:
        out = jax.ShapeDtypeStruct((rows // 4, width), f32)
        scratch = [pltpu.VMEM((rows, width), f32), pltpu.VMEM((rows, width), bf16)]
        scratch += [pltpu.VMEM((rows // 4 * 3, width // 2), bf16)] * 4
    found = pl.pallas_call(
        partial(comm_kernel, m, chain, kinds),
        out_shape=(out,) + tuple(jax.ShapeDtypeStruct(a.shape, a.dtype) for a in arrays),
        in_specs=[hbm] * (len(ins) + len(arrays)),
        out_specs=(vmem if scratch else hbm,) + (hbm,) * len(arrays),
        scratch_shapes=[
            pltpu.SemaphoreType.DMA((8 + len(kinds),)),
            pltpu.SemaphoreType.DMA((8 + len(kinds),)),
            pltpu.SemaphoreType.DMA,
        ]
        + scratch,
        compiler_params=pltpu.CompilerParams(
            collective_id=number, has_side_effects=True, vmem_limit_bytes=32 << 20
        ),
        name=chain,
    )(*ins, *arrays)
    first = found[0].reshape(-1, width) if not scratch else found[0]
    return (first,) + tuple(found[1:])


def rotate_in(values, cosine, sine_tab):
    half_dim = HEAD_DIM // 2
    front, back = values[:, :half_dim], values[:, half_dim:]
    return jnp.concatenate(
        [front * cosine - back * sine_tab, back * cosine + front * sine_tab], axis=1
    )


def qkv_kernel(heads, kv_heads, x_ref, gain_ref, w_ref, cos_ref, sin_ref, hidden_ref, q_ref, kv_ref):
    which = pl.program_id(0)

    @pl.when(which == 0)
    def _():
        values = x_ref[...].astype(f32)
        inverse = lax.rsqrt(jnp.mean(values * values, axis=1, keepdims=True) + norm_epsilon)
        hidden_ref[...] = (values * inverse * gain_ref[...]).astype(bf16)

    product = jnp.dot(
        hidden_ref[...], w_ref[...], preferred_element_type=f32
    )

    @pl.when(which < heads)
    def _():
        q_ref[...] = rotate_in(product, cos_ref[...], sin_ref[...]).astype(bf16)

    @pl.when((which >= heads) & (which < heads + kv_heads))
    def _():
        kv_ref[...] = rotate_in(product, cos_ref[...], sin_ref[...]).astype(bf16)

    @pl.when(which >= heads + kv_heads)
    def _():
        kv_ref[...] = product.astype(bf16)


def qkv_call(inputs, gain, mat, cosine, sine_tab, heads, kv_heads):
    rows, width = inputs.shape
    whole = lambda a: pl.BlockSpec(a.shape, lambda j: (0, 0))
    return pl.pallas_call(
        partial(qkv_kernel, heads, kv_heads),
        grid=(heads + 2 * kv_heads,),
        out_shape=(
            jax.ShapeDtypeStruct((rows, width), bf16),
            jax.ShapeDtypeStruct((rows, heads * HEAD_DIM), bf16),
            jax.ShapeDtypeStruct((rows, 2 * kv_heads * HEAD_DIM), bf16),
        ),
        in_specs=[
            whole(inputs),
            whole(gain),
            pl.BlockSpec((width, HEAD_DIM), lambda j: (0, j)),
            whole(cosine),
            whole(sine_tab),
        ],
        out_specs=(
            pl.BlockSpec((rows, width), lambda j: (0, 0)),
            pl.BlockSpec((rows, HEAD_DIM), lambda j: (0, jnp.minimum(j, heads - 1))),
            pl.BlockSpec((rows, HEAD_DIM), lambda j: (0, jnp.maximum(j - heads, 0))),
        ),
        compiler_params=pltpu.CompilerParams(vmem_limit_bytes=40 << 20),
        cost_estimate=pl.CostEstimate(flops=QKV_COST, bytes_accessed=0, transcendentals=0),
        name="qkv",
    )(inputs, gain, mat, cosine, sine_tab)


def scores_of(q, k_refs, low, first_row, kv_heads, head):
    rows, block = q.shape[0], k_refs[0].shape[0]
    last = len(k_refs) - 1
    query_at = last * block + first_row + lax.broadcasted_iota(jnp.int32, (rows, 1), 0)
    found = []
    for i, ref in enumerate(k_refs):
        raw = lax.dot_general(
            q, ref[...], (((1,), (1,)), ((), ())), preferred_element_type=f32
        )
        ratio = jnp.tanh(raw * (HEAD_DIM ** (-0.5) / softcap_limit))
        key_at = i * block + lax.broadcasted_iota(jnp.int32, (1, block), 1)
        found.append((ratio, (key_at >= low) & (key_at <= query_at)))
    return found


def attend_kernel(tile, q_ref, k2_ref, k1_ref, k0_ref, v2_ref, v1_ref, v0_ref, low_ref, o_ref, lse_ref):
    step = pl.program_id(1)
    k_refs, v_refs = (k2_ref, k1_ref, k0_ref), (v2_ref, v1_ref, v0_ref)
    found = scores_of(q_ref[...], k_refs, low_ref[...], step * tile, 1, 0)
    masked = [jnp.where(ok, softcap_limit * ratio, negative_fill) for ratio, ok in found]
    row_max = jnp.max(masked[0], axis=1, keepdims=True)
    for part in masked[1:]:
        row_max = jnp.maximum(row_max, jnp.max(part, axis=1, keepdims=True))
    exps = [jnp.exp(part - row_max) for part in masked]
    total = sum(jnp.sum(e, axis=1, keepdims=True) for e in exps)
    scale = 1.0 / total
    mixed = sum(
        jnp.dot((e * scale).astype(bf16), v[...], preferred_element_type=f32)
        for e, v in zip(exps, v_refs)
    )
    o_ref[...] = mixed.astype(bf16)
    lse_ref[0] = row_max + jnp.log(total)


def attend_call(query, window, low, heads, kv_heads):
    rows = query.shape[0]
    tile = rows // 3
    group = heads // kv_heads
    key = pl.BlockSpec((rows, HEAD_DIM), lambda h, i: (0, h // group))
    value = pl.BlockSpec((rows, HEAD_DIM), lambda h, i: (0, kv_heads + h // group))
    mine = pl.BlockSpec((tile, HEAD_DIM), lambda h, i: (i, h))
    return pl.pallas_call(
        partial(attend_kernel, tile),
        grid=(heads, rows // tile),
        out_shape=(
            jax.ShapeDtypeStruct(query.shape, bf16),
            jax.ShapeDtypeStruct((heads, rows, 1), f32),
        ),
        in_specs=[mine] + [key] * 3 + [value] * 3 + [pl.BlockSpec((tile, 1), lambda h, i: (i, 0))],
        out_specs=(mine, pl.BlockSpec((1, tile, 1), lambda h, i: (h, i, 0))),
        compiler_params=pltpu.CompilerParams(vmem_limit_bytes=48 << 20),
        cost_estimate=pl.CostEstimate(flops=ATTEND_COST, bytes_accessed=0, transcendentals=0),
        name="attend",
    )(query, *window, *window, low)


def attend_back_kernel(
    tile, q_ref, do_ref, k2_ref, k1_ref, k0_ref, v2_ref, v1_ref, v0_ref, low_ref, lse_ref, cos_ref, sin_ref,
    dq_ref, d2_ref, d1_ref, d0_ref, acc_ref,
):
    head, step = pl.program_id(0), pl.program_id(1)
    k_refs, v_refs = (k2_ref, k1_ref, k0_ref), (v2_ref, v1_ref, v0_ref)

    @pl.when((head == 0) & (step == 0))
    def _():
        acc_ref[...] = jnp.zeros_like(acc_ref)

    q, d_out = q_ref[...], do_ref[...]
    found = scores_of(q, k_refs, low_ref[...], step * tile, 1, 0)
    lse = lse_ref[0]
    probs = [jnp.where(ok, jnp.exp(softcap_limit * ratio - lse), 0.0) for ratio, ok in found]
    d_probs = [
        lax.dot_general(d_out, v[...], (((1,), (1,)), ((), ())), preferred_element_type=f32)
        for v in v_refs
    ]
    delta = sum(jnp.sum(p * d, axis=1, keepdims=True) for p, d in zip(probs, d_probs))
    d_query = 0.0
    for i, (p, d) in enumerate(zip(probs, d_probs)):
        ratio = found[i][0]
        d_raw = (p * (d - delta) * (1.0 - ratio * ratio) * (HEAD_DIM ** (-0.5))).astype(bf16)
        d_query += jnp.dot(d_raw, k_refs[i][...], preferred_element_type=f32)
        acc_ref[i, :, :HEAD_DIM] += contract_rows(d_raw, q)
        acc_ref[i, :, HEAD_DIM:] += contract_rows(p.astype(bf16), d_out)
    dq_ref[...] = rotate_in(d_query, cos_ref[...], -sin_ref[...]).astype(bf16)

    @pl.when((head == pl.num_programs(0) - 1) & (step == pl.num_programs(1) - 1))
    def _():
        d2_ref[...] = acc_ref[0].astype(bf16)
        d1_ref[...] = acc_ref[1].astype(bf16)
        d0_ref[...] = acc_ref[2]


def attend_back_call(query, d_out, window, low, lse, cosine, sine_tab, heads):
    rows = query.shape[0]
    tile = rows // 3
    key = pl.BlockSpec((rows, HEAD_DIM), lambda h, i: (0, 0))
    value = pl.BlockSpec((rows, HEAD_DIM), lambda h, i: (0, 1))
    mine = pl.BlockSpec((tile, HEAD_DIM), lambda h, i: (i, h))
    tab = pl.BlockSpec((tile, HEAD_DIM // 2), lambda h, i: (i, 0))
    back = pl.BlockSpec((rows, 2 * HEAD_DIM), lambda h, i: (0, 0))
    return pl.pallas_call(
        partial(attend_back_kernel, tile),
        grid=(heads, rows // tile),
        out_shape=(
            jax.ShapeDtypeStruct(query.shape, bf16),
            jax.ShapeDtypeStruct((rows, 2 * HEAD_DIM), bf16),
            jax.ShapeDtypeStruct((rows, 2 * HEAD_DIM), bf16),
            jax.ShapeDtypeStruct((rows, 2 * HEAD_DIM), f32),
        ),
        in_specs=[mine, mine]
        + [key] * 3
        + [value] * 3
        + [
            pl.BlockSpec((tile, 1), lambda h, i: (i, 0)),
            pl.BlockSpec((1, tile, 1), lambda h, i: (h, i, 0)),
            tab,
            tab,
        ],
        out_specs=(mine, back, back, back),
        scratch_shapes=[pltpu.VMEM((3, rows, 2 * HEAD_DIM), f32)],
        compiler_params=pltpu.CompilerParams(vmem_limit_bytes=56 << 20),
        cost_estimate=pl.CostEstimate(flops=ATTEND_BACK_COST, bytes_accessed=0, transcendentals=0),
        name="attend_back",
    )(query, d_out, *window, *window, low, lse, cosine, sine_tab)


def pick(array, index, axis=0):
    return lax.dynamic_index_in_dim(array, index, axis, keepdims=False)


class Order:
    def __init__(self, token):
        self.token = token

    def __call__(self, *values):
        values, self.token = lax.optimization_barrier((values, self.token))
        return values[0] if len(values) == 1 else values


def put(buffer, block, index):
    return lax.dynamic_update_index_in_dim(buffer, block, index, 0)


def local(
    inputs,
    seq_lengths,
    gain_attn_in,
    gain_attn_out,
    gain_ffn_in,
    gain_ffn_out,
    w_query,
    w_key,
    w_value,
    w_out,
    w_gate,
    w_up,
    w_down,
    out_grad,
):
    n = lax.axis_size("tok")
    m = n // 4
    width = inputs.shape[1]
    rows = inputs.shape[0]
    part = rows // 4
    tok = lax.axis_index("tok")
    tpi = lax.axis_index("tp")
    z, y = tok // m, tok % m
    zlo, zhi = z % 2, z // 2
    x, core = tpi // 2, tpi % 2
    wrows = w_query.shape[0]
    head_cols = w_query.shape[1]
    kv_cols = w_key.shape[1]
    heads = head_cols // HEAD_DIM
    kv_heads = kv_cols // HEAD_DIM
    units = w_gate.shape[1]
    half = units // 2

    def over_tok(fn):
        pairs = [(t, fn(t)) for t in range(n)]
        return lambda a: lax.ppermute(a, "tok", pairs)

    def over_tp(fn):
        pairs = [(t, fn(t)) for t in range(4)]
        return lambda a: lax.ppermute(a, "tp", pairs)

    def z_shift(a, k):
        return over_tok(lambda t: ((t // m + k) % 4) * m + t % m)(a)

    def y_shift(a, k):
        return over_tok(lambda t: (t // m) * m + (t % m + k) % m)(a)

    to_zlo = over_tok(lambda t: ((t // m) ^ 1) * m + t % m)
    to_zhi = over_tok(lambda t: ((t // m) ^ 2) * m + t % m)
    to_core = over_tp(lambda t: t ^ 1)
    to_x = over_tp(lambda t: t ^ 2)

    def within_quad(a, by):
        pairs = [(t, t + by) for t in range(n) if 0 <= t + by < n and t // QUAD == (t + by) // QUAD]
        return lax.ppermute(a, "tok", pairs)

    def place_of(dz, dy):
        return ((z ^ dz) * m) + (y - dy) % m

    step = Order(seq_lengths)

    def y_others(a):
        return [y_shift(a, j) for j in range(1, m)]

    def halves(a, index):
        return lax.dynamic_slice_in_dim(a, index * half, half, 1)

    attn_own = jnp.concatenate([w_query, w_key, w_value, w_out], axis=1)
    gains = jnp.concatenate([gain_attn_in, gain_attn_out, gain_ffn_in, gain_ffn_out])
    attn_cols = attn_own.shape[1]
    gains = jnp.pad(gains, (0, attn_cols - gains.shape[0])).reshape(1, attn_cols)
    attn_own = jnp.concatenate([attn_own, jnp.pad(gains, ((0, 15), (0, 0)))], axis=0)
    gu_keep = jnp.concatenate([halves(w_gate, zlo), halves(w_up, zlo)], axis=1)
    gu_send = jnp.concatenate([halves(w_gate, 1 - zlo), halves(w_up, 1 - zlo)], axis=1)
    d_keep, d_send = halves(w_down, zlo), halves(w_down, 1 - zlo)
    own_index = tok * rows + jnp.arange(rows, dtype=jnp.int32)
    seq_start = sequence_start(seq_lengths, own_index)
    cosine, sine_tab = rope_tables(own_index - seq_start)
    low = (seq_start - (tok - REACH) * rows)[:, None]
    attn_own, cosine, sine_tab, low = step(attn_own, cosine, sine_tab, low)
    attn_buf, gu_buf, d_buf = gather_call(n, attn_own, gu_keep, gu_send, d_keep, d_send)
    gu_z = {k: pick(gu_buf, (z ^ k) * m + y) for k in (1, 2)}
    d_z = {0: d_keep, 1: pick(d_buf, (z ^ 1) * m + y)}

    gains_all = attn_buf[:, wrows, : 4 * wrows].reshape(n, 4, wrows)
    gains_all = gains_all.transpose(1, 0, 2).reshape(4, 1, width).astype(f32)
    gain_one, gain_two, gain_three, gain_four = (gains_all[i] for i in range(4))

    def own_slice(a):
        return lax.dynamic_slice_in_dim(a, tpi * part, part, 0)

    def gather_tp(a):
        buffer = jnp.zeros((4,) + a.shape, a.dtype)
        low = a.astype(bf16)
        other = to_x(low)
        pair = to_core(jnp.stack([low, other]))
        for k, block in enumerate((a, pair[0], other, pair[1])):
            buffer = put(buffer, block.astype(a.dtype), tpi ^ k)
        return buffer.reshape((-1,) + a.shape[1:])

    def reduce_tp(compute):
        far = compute(1 - core).astype(bf16)
        near = compute(core) + to_core(far).astype(f32)
        near = near.reshape(2, part, width)
        return pick(near, x) + to_x(pick(near, 1 - x).astype(bf16)).astype(f32)

    def core_rows(a, c):
        return pick(a.reshape(2, 2, part, a.shape[1]), c, 1).reshape(2 * part, a.shape[1])

    qkv_cols = head_cols + 2 * kv_cols
    qkv_mat = attn_buf[:, :wrows, :qkv_cols].reshape(width, qkv_cols)
    out_mat = attn_buf[:, :wrows, qkv_cols:].reshape(width, head_cols)
    hidden_one, query, key_value = qkv_call(
        inputs, gain_one, qkv_mat, cosine, sine_tab, heads, kv_heads
    )
    window = [within_quad(key_value, by) for by in range(REACH, 0, -1)] + [key_value]
    attended, lse = attend_call(query, window, low, heads, kv_heads)
    far, near = (contract_cols(core_rows(attended, c), out_mat) for c in (1 - core, core))
    def over_y(a):
        return [(a, ("y", j)) for j in range(1, m)]

    attn, gu3, *arrived = comm_call(
        n, 1, "reduce_tp", (far.astype(bf16), near), [(gu_z[1], ("zhi",))] + over_y(gu_z[1]) + over_y(gu_z[2])
    )
    gu_z[3] = gu3
    gu_y = {1: arrived[: m - 1], 2: arrived[m - 1 :]}

    resid = own_slice(inputs).astype(f32)
    unit_two, inv_two = norm_parts(attn)
    resid_mid = resid + unit_two * gain_two
    unit_three, inv_three = norm_parts(resid_mid)
    def fill(buffer, by_z, by_y):
        for k in by_z:
            buffer = put(buffer, by_z[k], (z ^ k) * m + y)
        for k in by_y:
            for j, piece in enumerate(by_y[k]):
                buffer = put(buffer, piece, (z ^ k) * m + (y - j - 1) % m)
        return buffer

    hidden_two = (unit_three * gain_three).astype(bf16)
    hidden_two, d2, d3, *arrived = comm_call(
        n,
        2,
        "gather_pair",
        (hidden_two,),
        [(d_z[0], ("zhi",)), (d_z[1], ("zhi",))] + over_y(gu_z[3]) + over_y(d_z[0]) + over_y(d_z[1]),
    )
    gu_y[3] = arrived[: m - 1]
    d_y = {0: arrived[m - 1 : 2 * m - 2], 1: arrived[2 * m - 2 :]}
    d_z[2], d_z[3] = d2, d3
    d_y[2], d_y[3] = y_others(d2), y_others(d3)
    gu_mat = fill(gu_buf, {3: gu_z[3]}, gu_y).reshape(width, -1)
    down_mat = fill(d_buf, {2: d_z[2], 3: d_z[3]}, d_y).reshape(width, -1)
    gate_up = jnp.dot(hidden_two, gu_mat, preferred_element_type=f32)
    gate_vals, up_vals = gate_up[:, :half], gate_up[:, half:]
    activated, gelu_pull = jax.vjp(partial(jax.nn.gelu, approximate=True), gate_vals)
    inner = (activated * up_vals).astype(bf16)
    inner_far, inner_near = inner[2 * rows // 2 :], inner[: 2 * rows // 2]
    (ffn,) = comm_call(
        n, 3, "reduce_pair", (contract_cols(inner_far, down_mat).astype(bf16), contract_cols(inner_near, down_mat))
    )
    unit_four, inv_four = norm_parts(ffn)
    layer_out = gather_tp((resid_mid + unit_four * gain_four).astype(bf16))

    grad_out = own_slice(out_grad).astype(f32)
    d_ffn, grad_four = norm_back(grad_out, gain_four, unit_four, inv_four)
    (d_ffn_all,) = comm_call(n, 4, "gather_pair", (d_ffn.astype(bf16),))
    d_inner = jnp.dot(d_ffn_all, down_mat, preferred_element_type=f32)

    def y_send(grad):
        blocks = grad.astype(bf16).reshape(4, m, wrows, -1)
        return [pick(blocks, y, 1)] + [y_shift(pick(blocks, (y + j) % m, 1), j) for j in range(1, m)]

    def add_up(terms):
        return sum(t.astype(f32) for t in terms)

    def zhi_send(terms):
        total = add_up(terms).reshape(2, 2, wrows, -1)
        return [pick(total, zhi), to_zhi(pick(total, 1 - zhi).astype(bf16))]

    def zlo_send(terms):
        total = add_up(terms)
        return pick(total, zlo), to_zlo(pick(total, 1 - zlo).astype(bf16)).astype(f32)

    def z_send(terms):
        total = add_up(terms)
        return [pick(total, z)] + [
            z_shift(pick(total, (z + k) % 4).astype(bf16), k) for k in range(1, 4)
        ]

    def sides(own, other):
        return jnp.where(
            zlo == 0,
            jnp.concatenate([own, other], axis=1),
            jnp.concatenate([other, own], axis=1),
        )

    down_s = y_send(contract_rows(d_ffn_all, inner))
    grad_upvals = (d_inner * activated).astype(bf16)
    grad_gatevals = gelu_pull(d_inner * up_vals)[0].astype(bf16)
    grad_gu = jnp.concatenate([grad_gatevals, grad_upvals], axis=1)
    far, near = (contract_cols(jnp.split(grad_gu, 2)[k], gu_mat) for k in (1, 0))
    near = near + to_core(far.astype(bf16)).astype(f32)
    near = near.reshape(2, 2, part, width)
    mid = width // 2
    left, right = near[..., :mid], near[..., mid:]
    left_in, right_in = to_x(left[1].astype(bf16)), to_zlo(right[:, 1].astype(bf16))
    gate_s = y_send(contract_rows(hidden_two, grad_gatevals))
    up_s = y_send(contract_rows(hidden_two, grad_upvals))
    left_in, right_in = step(left_in, right_in)
    left = left[0] + left_in.astype(f32)
    right = right[:, 0] + right_in.astype(f32)
    left_in, right_in = to_zlo(left[1].astype(bf16)), to_x(right[1].astype(bf16))
    down_s = step(down_s)
    left_in, right_in = step(left_in, right_in)
    d_hidden_two = jnp.concatenate(
        [left[0] + left_in.astype(f32), right[0] + right_in.astype(f32)], axis=1
    )
    down_s = zhi_send(down_s)

    mid_add, grad_three = norm_back(d_hidden_two, gain_three, unit_three, inv_three)
    d_mid = grad_out + mid_add

    d_attn, grad_two = norm_back(d_mid, gain_two, unit_two, inv_two)
    d_attn_low = gather_tp(d_attn.astype(bf16))

    d_attn_low = step(d_attn_low)
    wout_s = contract_rows(d_attn_low, attended)
    d_attended = jnp.dot(d_attn_low, out_mat, preferred_element_type=f32).astype(bf16)
    gate_s, down_s = step(gate_s, down_s)
    gate_s = zhi_send(gate_s)
    d_query, *d_window, d_kv = attend_back_call(
        query, d_attended, window, low, lse, cosine, sine_tab, heads
    )
    d_window = [within_quad(d_window[REACH - by], -by) for by in range(1, REACH + 1)]
    q_grad = contract_rows(hidden_one, d_query)
    up_s, wout_s = step(up_s, wout_s)
    up_s, wout_s = zhi_send(up_s), y_send(wout_s)
    out_down = sides(*zlo_send(down_s))
    d_window = step(d_window)
    q_s = y_send(q_grad)
    d_kv = d_kv + add_up(d_window)
    d_key = rotate_in(d_kv[:, :kv_cols], cosine, -sine_tab)
    d_key_value = jnp.concatenate([d_key.astype(bf16), d_kv[:, kv_cols:].astype(bf16)], axis=1)
    d_qkv = jnp.concatenate([d_query, d_key_value], axis=1)
    kv_s = y_send(contract_rows(hidden_one, d_key_value))
    d_hidden_one = reduce_tp(lambda c: contract_cols(core_rows(d_qkv, c), qkv_mat))
    unit_one, inv_one = norm_parts(resid)
    input_add, grad_one = norm_back(d_hidden_one, gain_one, unit_one, inv_one)
    gate_s = step(gate_s)
    out_gate = sides(*zlo_send(gate_s))
    wout_s = z_send(step(wout_s))
    up_s = step(up_s)
    out_up = sides(*zlo_send(up_s))
    q_s = z_send(step(q_s))
    kv_s = z_send(step(kv_s))
    out_wout, out_q, out_kv = add_up(wout_s), add_up(q_s), add_up(kv_s)
    input_grad = gather_tp(d_mid + input_add)

    gain_grads = jnp.stack([grad_one, grad_two, grad_three, grad_four])
    gain_grads = gain_grads + to_core(gain_grads)
    gain_grads = gain_grads + to_x(gain_grads)
    bit = 1
    while bit < n:
        gain_grads = gain_grads + over_tok(lambda t: t ^ bit)(gain_grads)
        bit *= 2
    gain_grads = lax.dynamic_slice_in_dim(gain_grads, tok * wrows, wrows, 1)
    return (
        layer_out,
        input_grad,
        gain_grads[0],
        gain_grads[1],
        gain_grads[2],
        gain_grads[3],
        out_q,
        out_kv[:, :kv_cols],
        out_kv[:, kv_cols:],
        out_wout,
        out_gate,
        out_up,
        out_down,
    )


def solution(mesh):
    weight = P("tok", "tp")
    in_specs = (P("tok", None), P()) + (P("tok"),) * 4 + (weight,) * 7 + (P("tok", None),)
    out_specs = (P("tok", None),) * 2 + (P("tok"),) * 4 + (weight,) * 7
    return jax.shard_map(local, mesh=mesh, in_specs=in_specs, out_specs=out_specs, check_vma=False)
```

```python
from functools import partial

import jax
import jax.numpy as jnp
from jax import lax
from jax.experimental import pallas as pl
from jax.experimental.pallas import tpu as pltpu
from jax.sharding import PartitionSpec as P

HEAD_DIM = 256
QUAD = 4
REACH = 2

softcap_limit = 50.0
norm_epsilon = 1e-06
rope_base = 10000.0
negative_fill = -1e30

QKV_COST = 10_000_000_000
ATTEND_COST = 20_000_000_000
ATTEND_BACK_COST = 40_000_000_000

f32 = jnp.float32
bf16 = jnp.bfloat16


def norm_parts(values):
    inverse = lax.rsqrt(jnp.mean(values * values, axis=-1, keepdims=True) + norm_epsilon)
    return values * inverse, inverse


def norm_back(gradient, gain_vec, unit_vals, inverse):
    scaled = gradient * gain_vec
    input_part = inverse * (
        scaled - unit_vals * jnp.mean(scaled * unit_vals, axis=-1, keepdims=True)
    )
    return (input_part, jnp.sum(gradient * unit_vals, axis=0))


def sequence_start(seq_lengths, tok_index):
    count = seq_lengths.shape[0]
    before = jnp.arange(count)[:, None] > jnp.arange(count)[None, :]
    starts = jnp.sum(jnp.where(before, seq_lengths[None, :], 0), axis=1)
    passed = tok_index[:, None] >= starts[None, :]
    return jnp.max(jnp.where(passed, starts[None, :], 0), axis=1)


def rope_tables(position):
    half_dim = HEAD_DIM // 2
    freqs = rope_base ** (-2.0 * jnp.arange(half_dim).astype(f32) / HEAD_DIM)
    theta = position.astype(f32)[:, None] * freqs[None, :]
    return (jnp.cos(theta), jnp.sin(theta))


def contract_rows(left, right):
    return lax.dot_general(
        left, right, (((0,), (0,)), ((), ())), preferred_element_type=f32
    )


def contract_cols(left, right):
    return lax.dot_general(
        left, right, (((1,), (1,)), ((), ())), preferred_element_type=f32
    )


def gather_kernel(
    m, attn_ref, guk_ref, gus_ref, dk_ref, ds_ref, attn_buf, gu_buf, d_buf, send_sem, recv_sem, own_sem
):
    tok, tp = lax.axis_index("tok"), lax.axis_index("tp")
    z, y = tok // m, tok % m
    flip1 = z + 1 - 2 * (z % 2)
    flip2 = (z + 2) % 4
    flip3 = 3 - z
    slot = lambda zs, ys: zs * m + ys
    others = range(1, m)
    used = iter(range(9 + 8 * (m - 1)))

    def hop(src, dst, number, target):
        return pltpu.make_async_remote_copy(
            src_ref=src,
            dst_ref=dst,
            send_sem=send_sem.at[number],
            recv_sem=recv_sem.at[number],
            device_id=(target, tp),
            device_id_type=pl.DeviceIdType.MESH,
        )

    barrier = pltpu.get_barrier_semaphore()
    peers = [slot(f, y) for f in (flip1, flip2, flip3)] + [slot(z, (y + j) % m) for j in others]
    for peer in peers:
        pl.semaphore_signal(barrier, inc=1, device_id=(peer, tp), device_id_type=pl.DeviceIdType.MESH)
    pl.semaphore_wait(barrier, len(peers))

    own = [
        pltpu.make_async_copy(src, dst.at[tok], own_sem.at[i])
        for i, (src, dst) in enumerate(((attn_ref, attn_buf), (guk_ref, gu_buf), (dk_ref, d_buf)))
    ]
    ups = [next(used) for _ in range(3)]
    downs = [next(used) for _ in range(3)]
    y_own = {j: next(used) for j in others}
    y_gu = {j: next(used) for j in others}
    y_up = {(s, j): next(used) for s in (1, 2, 3) for j in others}
    y_down = {(s, j): next(used) for s in (1, 2, 3) for j in others}
    n_gu1, n_d1, n_gu2 = next(used), next(used), next(used)

    def line(step, way):
        at = slot(z - way * (step - 1), y)
        src = attn_ref if step == 1 else attn_buf.at[at]
        return hop(src, attn_buf.at[at], (ups if way > 0 else downs)[step - 1], slot(z + way, y))

    def can_send(step, way):
        return (z >= step - 1) & (z <= 2) if way > 0 else (z <= 4 - step) & (z >= 1)

    def can_take(step, way):
        return z >= step if way > 0 else z <= 3 - step

    def taken(step, way):
        at = slot(z - way * step, y)
        return hop(attn_buf.at[at], attn_buf.at[at], (ups if way > 0 else downs)[step - 1], tok)

    def relay(step, way, j, back):
        at = slot(z - way * step, (y - j) % m if back else y)
        number = (y_up if way > 0 else y_down)[step, j]
        return hop(attn_buf.at[at], attn_buf.at[at], number, slot(z, (y + j) % m))

    y_own_hops = [hop(attn_ref, attn_buf.at[tok], y_own[j], slot(z, (y + j) % m)) for j in others]
    y_gu_hops = [hop(guk_ref, gu_buf.at[tok], y_gu[j], slot(z, (y + j) % m)) for j in others]
    z_hops = [
        hop(gus_ref, gu_buf.at[tok], n_gu1, slot(flip1, y)),
        hop(guk_ref, gu_buf.at[tok], n_gu2, slot(flip2, y)),
        hop(ds_ref, d_buf.at[tok], n_d1, slot(flip1, y)),
    ]

    for way in (1, -1):
        pl.when(can_send(1, way))(line(1, way).start)
    for c in y_own_hops + y_gu_hops + own:
        c.start()
    for step in (1, 2, 3):
        for way in (1, -1):

            @pl.when(can_take(step, way))
            def _(step=step, way=way):
                taken(step, way).wait_recv()
                if step < 3:
                    pl.when(can_send(step + 1, way))(line(step + 1, way).start)
                for j in others:
                    relay(step, way, j, False).start()

        if step == 2:
            for c in z_hops:
                c.start()
    for j in others:
        at = slot(z, (y - j) % m)
        hop(attn_buf.at[at], attn_buf.at[at], y_own[j], tok).wait_recv()
        hop(gu_buf.at[at], gu_buf.at[at], y_gu[j], tok).wait_recv()
    for step in (1, 2, 3):
        for way in (1, -1):

            @pl.when(can_take(step, way))
            def _(step=step, way=way):
                for j in others:
                    relay(step, way, j, True).wait_recv()
                    relay(step, way, j, False).wait_send()

            pl.when(can_send(step, way))(line(step, way).wait_send)
    for number, ref, f in ((n_gu1, gu_buf, flip1), (n_d1, d_buf, flip1), (n_gu2, gu_buf, flip2)):
        at = slot(f, y)
        hop(ref.at[at], ref.at[at], number, tok).wait_recv()
    for c in y_own_hops + y_gu_hops + z_hops:
        c.wait_send()
    for c in own:
        c.wait()


def gather_call(n, attn, gu_keep, gu_send, d_keep, d_send):
    m = n // 4
    count = 9 + 8 * (m - 1)
    hbm = pl.BlockSpec(memory_space=pltpu.HBM)
    return pl.pallas_call(
        partial(gather_kernel, m),
        out_shape=tuple(jax.ShapeDtypeStruct((n,) + a.shape, bf16) for a in (attn, gu_keep, d_keep)),
        in_specs=[hbm] * 5,
        out_specs=(hbm,) * 3,
        scratch_shapes=[
            pltpu.SemaphoreType.DMA((count,)),
            pltpu.SemaphoreType.DMA((count,)),
            pltpu.SemaphoreType.DMA((3,)),
        ],
        compiler_params=pltpu.CompilerParams(collective_id=0, has_side_effects=True),
        name="gather_first",
    )(attn, gu_keep, gu_send, d_keep, d_send)


def tie_kernel(*refs):
    del refs


def tie(values, *earlier):
    leaves, tree = jax.tree.flatten(values)
    earlier = jax.tree.leaves(earlier)
    anywhere = pl.BlockSpec(memory_space=pl.ANY)
    found = pl.pallas_call(
        tie_kernel,
        out_shape=tuple(jax.ShapeDtypeStruct(v.shape, v.dtype) for v in leaves),
        in_specs=[anywhere] * (len(leaves) + len(earlier)),
        out_specs=(anywhere,) * len(leaves),
        input_output_aliases={i: i for i in range(len(leaves))},
        name="tie",
    )(*leaves, *earlier)
    return jax.tree.unflatten(tree, found)


def add_rows(total_ref, arrived_ref):
    block = 32 if total_ref.shape[0] % 32 == 0 else total_ref.shape[0]

    def body(i, carry):
        at = pl.ds(pl.multiple_of(i * block, block), block)
        total_ref[at, :] = total_ref[at, :] + arrived_ref[at, :].astype(f32)
        return carry

    lax.fori_loop(0, total_ref.shape[0] // block, body, 0)


def round_rows(out_ref, value_ref):
    block = 32 if out_ref.shape[0] % 32 == 0 else out_ref.shape[0]

    def body(i, carry):
        at = pl.ds(pl.multiple_of(i * block, block), block)
        out_ref[at, :] = value_ref[at, :].astype(out_ref.dtype)
        return carry

    lax.fori_loop(0, out_ref.shape[0] // block, body, 0)


def comm_kernel(m, chain, kinds, *refs):
    count = {"gather_pair": 1, "gather_tp": 1, "reduce_pair": 2, "reduce_tp": 2}[chain]
    ins, refs = refs[:count], refs[count:]
    sent, refs = refs[: len(kinds)], refs[len(kinds) :]
    out_ref, refs = refs[0], refs[1:]
    landed, refs = refs[: len(kinds)], refs[len(kinds) :]
    send_sem, recv_sem, own_sem = refs[:3]
    scratch = refs[3:]
    tok, tp = lax.axis_index("tok"), lax.axis_index("tp")
    z, y = tok // m, tok % m
    x, c = tp // 2, tp % 2
    others = range(1, m)
    zlo = ((z + 1 - 2 * (z % 2)) * m + y, tp)
    zhi = (((z + 2) % 4) * m + y, tp)
    over_x, over_core = (tok, (tp + 2) % 4), (tok, tp + 1 - 2 * c)
    used = iter(range(8 + len(kinds)))

    def hop(src, dst, target):
        number = next(used)
        return pltpu.make_async_remote_copy(
            src_ref=src,
            dst_ref=dst,
            send_sem=send_sem.at[number],
            recv_sem=recv_sem.at[number],
            device_id=target,
            device_id_type=pl.DeviceIdType.MESH,
        )

    def target(kind):
        if kind[0] == "y":
            return (z * m + (y + kind[1]) % m, tp)
        return {"zlo": zlo, "zhi": zhi}[kind[0]]

    peers = [over_x, over_core]
    if chain in ("gather_pair", "reduce_pair") or ("zlo",) in kinds:
        peers.append(zlo)
    if ("zhi",) in kinds:
        peers.append(zhi)
    if any(kind[0] == "y" for kind in kinds):
        peers += [(z * m + (y + j) % m, tp) for j in others]
    barrier = pltpu.get_barrier_semaphore()
    for peer in peers:
        pl.semaphore_signal(barrier, inc=1, device_id=peer, device_id_type=pl.DeviceIdType.MESH)
    pl.semaphore_wait(barrier, len(peers))

    beside = [hop(a, b, target(kind)) for a, b, kind in zip(sent, landed, kinds)]
    waits = []

    def start_beside():
        for b in beside:
            b.start()

    if chain == "gather_tp":
        (a_ref,) = ins
        own = pltpu.make_async_copy(a_ref, out_ref.at[tp], own_sem)
        there = (tp + 2) % 4
        first = hop(a_ref, out_ref.at[tp], over_x)
        near = hop(a_ref, out_ref.at[tp], over_core)
        far = hop(out_ref.at[there], out_ref.at[there], over_core)
        first.start()
        start_beside()
        near.start()
        own.start()
        first.wait_recv()
        far.start()
        near.wait_recv()
        far.wait_recv()
        own.wait()
        waits = [first, near, far]
    elif chain == "gather_pair":
        (a_ref,) = ins
        half = a_ref.shape[0] // 2
        top, low = pl.ds(0, half), pl.ds(half, half)
        own = pltpu.make_async_copy(a_ref, out_ref.at[0], own_sem)
        first_z = hop(a_ref, out_ref.at[1], zlo)
        first_x = hop(a_ref, out_ref.at[2], over_x)
        next_x = hop(out_ref.at[1, top], out_ref.at[3, top], over_x)
        next_z = hop(out_ref.at[2, low], out_ref.at[3, low], zlo)
        core = [
            hop(a_ref if k == 0 else out_ref.at[k], out_ref.at[4 + k], over_core) for k in range(4)
        ]
        first_z.start()
        first_x.start()
        own.start()
        core[0].start()
        start_beside()
        first_z.wait_recv()
        next_x.start()
        core[1].start()
        first_x.wait_recv()
        next_z.start()
        core[2].start()
        next_x.wait_recv()
        next_z.wait_recv()
        core[3].start()
        for each in core:
            each.wait_recv()
        own.wait()
        waits = [first_z, first_x, next_x, next_z] + core
    elif chain == "reduce_tp":
        far_ref, near_ref = ins
        near, from_core, to_go, from_x = scratch
        part = out_ref.shape[0]
        own = pltpu.make_async_copy(near_ref, near, own_sem)
        core = hop(far_ref, from_core, over_core)
        over = hop(to_go, from_x, over_x)
        core.start()
        own.start()
        start_beside()
        own.wait()
        core.wait_recv()
        away = pl.ds(pl.multiple_of((1 - x) * part, part), part)
        here = pl.ds(pl.multiple_of(x * part, part), part)
        add_rows(near.at[away], from_core.at[away])
        round_rows(to_go, near.at[away])
        over.start()
        add_rows(near.at[here], from_core.at[here])
        round_rows(out_ref, near.at[here])
        over.wait_recv()
        add_rows(out_ref, from_x)
        waits = [core, over]
    else:
        far_ref, near_ref = ins
        near, from_core, left_go, left_in, right_go, right_in = scratch
        part, width = out_ref.shape
        mid = width // 2
        left, right = pl.ds(0, mid), pl.ds(mid, mid)
        rows = lambda k, count=1: pl.ds(k * part, count * part)
        own = pltpu.make_async_copy(near_ref, near, own_sem)
        core = hop(far_ref, from_core, over_core)
        left_x = hop(left_go.at[rows(0, 2)], left_in.at[rows(0, 2)], over_x)
        right_z = hop(right_go.at[rows(0, 2)], right_in.at[rows(0, 2)], zlo)
        left_z = hop(left_go.at[rows(2)], left_in.at[rows(2)], zlo)
        right_x = hop(right_go.at[rows(2)], right_in.at[rows(2)], over_x)
        core.start()
        own.start()
        start_beside()
        own.wait()
        core.wait_recv()
        add_rows(near.at[rows(1, 3)], from_core.at[rows(1, 3)])
        round_rows(left_go.at[rows(0, 2)], near.at[rows(2, 2), left])
        left_x.start()
        round_rows(right_go.at[rows(0)], near.at[rows(1), right])
        round_rows(right_go.at[rows(1)], near.at[rows(3), right])
        right_z.start()
        add_rows(near.at[rows(0)], from_core.at[rows(0)])
        left_x.wait_recv()
        add_rows(near.at[rows(0, 2), left], left_in.at[rows(0, 2)])
        round_rows(left_go.at[rows(2)], near.at[rows(1), left])
        left_z.start()
        right_z.wait_recv()
        add_rows(near.at[rows(0), right], right_in.at[rows(0)])
        add_rows(near.at[rows(2), right], right_in.at[rows(1)])
        round_rows(right_go.at[rows(2)], near.at[rows(2), right])
        right_x.start()
        round_rows(out_ref, near.at[rows(0)])
        left_z.wait_recv()
        add_rows(out_ref.at[:, left], left_in.at[rows(2)])
        right_x.wait_recv()
        add_rows(out_ref.at[:, right], right_in.at[rows(2)])
        waits = [core, left_x, right_z, left_z, right_x]
    for each in waits:
        each.wait_send()
    for b in beside:
        b.wait_recv()
        b.wait_send()


def comm_call(n, number, chain, ins, beside=()):
    m = n // 4
    kinds = tuple(kind for _, kind in beside)
    arrays = [a for a, _ in beside]
    hbm = pl.BlockSpec(memory_space=pltpu.HBM)
    vmem = pl.BlockSpec(memory_space=pltpu.VMEM)
    rows, width = ins[-1].shape
    scratch = []
    if chain == "gather_tp":
        out = jax.ShapeDtypeStruct((4, rows, width), bf16)
    elif chain == "gather_pair":
        out = jax.ShapeDtypeStruct((8, rows, width), bf16)
    elif chain == "reduce_tp":
        out = jax.ShapeDtypeStruct((rows // 2, width), f32)
        scratch = [
            pltpu.VMEM((rows, width), f32),
            pltpu.VMEM((rows, width), bf16),
            pltpu.VMEM((rows // 2, width), bf16),
            pltpu.VMEM((rows // 2, width), bf16),
        ]
    else:
        out = jax.ShapeDtypeStruct((rows // 4, width), f32)
        scratch = [pltpu.VMEM((rows, width), f32), pltpu.VMEM((rows, width), bf16)]
        scratch += [pltpu.VMEM((rows // 4 * 3, width // 2), bf16)] * 4
    found = pl.pallas_call(
        partial(comm_kernel, m, chain, kinds),
        out_shape=(out,) + tuple(jax.ShapeDtypeStruct(a.shape, a.dtype) for a in arrays),
        in_specs=[hbm] * (len(ins) + len(arrays)),
        out_specs=(vmem if scratch else hbm,) + (hbm,) * len(arrays),
        scratch_shapes=[
            pltpu.SemaphoreType.DMA((8 + len(kinds),)),
            pltpu.SemaphoreType.DMA((8 + len(kinds),)),
            pltpu.SemaphoreType.DMA,
        ]
        + scratch,
        compiler_params=pltpu.CompilerParams(
            collective_id=number, has_side_effects=True, vmem_limit_bytes=32 << 20
        ),
        name=chain,
    )(*ins, *arrays)
    first = found[0].reshape(-1, width) if not scratch else found[0]
    return (first,) + tuple(found[1:])


def rotate_in(values, cosine, sine_tab):
    half_dim = HEAD_DIM // 2
    front, back = values[:, :half_dim], values[:, half_dim:]
    return jnp.concatenate(
        [front * cosine - back * sine_tab, back * cosine + front * sine_tab], axis=1
    )


def qkv_kernel(heads, kv_heads, x_ref, gain_ref, w_ref, cos_ref, sin_ref, hidden_ref, q_ref, kv_ref):
    which = pl.program_id(0)

    @pl.when(which == 0)
    def _():
        values = x_ref[...].astype(f32)
        inverse = lax.rsqrt(jnp.mean(values * values, axis=1, keepdims=True) + norm_epsilon)
        hidden_ref[...] = (values * inverse * gain_ref[...]).astype(bf16)

    product = jnp.dot(
        hidden_ref[...], w_ref[...].reshape(-1, HEAD_DIM), preferred_element_type=f32
    )

    @pl.when(which < heads)
    def _():
        q_ref[...] = rotate_in(product, cos_ref[...], sin_ref[...]).astype(bf16)

    @pl.when((which >= heads) & (which < heads + kv_heads))
    def _():
        kv_ref[...] = rotate_in(product, cos_ref[...], sin_ref[...]).astype(bf16)

    @pl.when(which >= heads + kv_heads)
    def _():
        kv_ref[...] = product.astype(bf16)


def qkv_call(inputs, gain, mat, cosine, sine_tab, heads, kv_heads):
    rows, width = inputs.shape
    n = mat.shape[0]
    whole = lambda a: pl.BlockSpec(a.shape, lambda j: (0, 0))
    return pl.pallas_call(
        partial(qkv_kernel, heads, kv_heads),
        grid=(heads + 2 * kv_heads,),
        out_shape=(
            jax.ShapeDtypeStruct((rows, width), bf16),
            jax.ShapeDtypeStruct((rows, heads * HEAD_DIM), bf16),
            jax.ShapeDtypeStruct((rows, 2 * kv_heads * HEAD_DIM), bf16),
        ),
        in_specs=[
            whole(inputs),
            whole(gain),
            pl.BlockSpec((n, width // n, HEAD_DIM), lambda j: (0, 0, j)),
            whole(cosine),
            whole(sine_tab),
        ],
        out_specs=(
            pl.BlockSpec((rows, width), lambda j: (0, 0)),
            pl.BlockSpec((rows, HEAD_DIM), lambda j: (0, jnp.minimum(j, heads - 1))),
            pl.BlockSpec((rows, HEAD_DIM), lambda j: (0, jnp.maximum(j - heads, 0))),
        ),
        compiler_params=pltpu.CompilerParams(vmem_limit_bytes=40 << 20),
        cost_estimate=pl.CostEstimate(flops=QKV_COST, bytes_accessed=0, transcendentals=0),
        name="qkv",
    )(inputs, gain, mat, cosine, sine_tab)


def scores_of(q, k_refs, low, first_row, kv_heads, head):
    rows, block = q.shape[0], k_refs[0].shape[0]
    last = len(k_refs) - 1
    query_at = last * block + first_row + lax.broadcasted_iota(jnp.int32, (rows, 1), 0)
    found = []
    for i, ref in enumerate(k_refs):
        raw = lax.dot_general(
            q, ref[...], (((1,), (1,)), ((), ())), preferred_element_type=f32
        )
        ratio = jnp.tanh(raw * (HEAD_DIM ** (-0.5) / softcap_limit))
        key_at = i * block + lax.broadcasted_iota(jnp.int32, (1, block), 1)
        found.append((ratio, (key_at >= low) & (key_at <= query_at)))
    return found


def attend_kernel(tile, q_ref, k2_ref, k1_ref, k0_ref, v2_ref, v1_ref, v0_ref, low_ref, o_ref, lse_ref):
    step = pl.program_id(1)
    k_refs, v_refs = (k2_ref, k1_ref, k0_ref), (v2_ref, v1_ref, v0_ref)
    found = scores_of(q_ref[...], k_refs, low_ref[...], step * tile, 1, 0)
    masked = [jnp.where(ok, softcap_limit * ratio, negative_fill) for ratio, ok in found]
    row_max = jnp.max(masked[0], axis=1, keepdims=True)
    for part in masked[1:]:
        row_max = jnp.maximum(row_max, jnp.max(part, axis=1, keepdims=True))
    exps = [jnp.exp(part - row_max) for part in masked]
    total = sum(jnp.sum(e, axis=1, keepdims=True) for e in exps)
    scale = 1.0 / total
    mixed = sum(
        jnp.dot((e * scale).astype(bf16), v[...], preferred_element_type=f32)
        for e, v in zip(exps, v_refs)
    )
    o_ref[...] = mixed.astype(bf16)
    lse_ref[0] = row_max + jnp.log(total)


def attend_call(query, window, low, heads, kv_heads):
    rows = query.shape[0]
    tile = rows // 3
    group = heads // kv_heads
    key = pl.BlockSpec((rows, HEAD_DIM), lambda h, i: (0, h // group))
    value = pl.BlockSpec((rows, HEAD_DIM), lambda h, i: (0, kv_heads + h // group))
    mine = pl.BlockSpec((tile, HEAD_DIM), lambda h, i: (i, h))
    return pl.pallas_call(
        partial(attend_kernel, tile),
        grid=(heads, rows // tile),
        out_shape=(
            jax.ShapeDtypeStruct(query.shape, bf16),
            jax.ShapeDtypeStruct((heads, rows, 1), f32),
        ),
        in_specs=[mine] + [key] * 3 + [value] * 3 + [pl.BlockSpec((tile, 1), lambda h, i: (i, 0))],
        out_specs=(mine, pl.BlockSpec((1, tile, 1), lambda h, i: (h, i, 0))),
        compiler_params=pltpu.CompilerParams(vmem_limit_bytes=48 << 20),
        cost_estimate=pl.CostEstimate(flops=ATTEND_COST, bytes_accessed=0, transcendentals=0),
        name="attend",
    )(query, *window, *window, low)


def attend_back_kernel(
    tile, q_ref, do_ref, k2_ref, k1_ref, k0_ref, v2_ref, v1_ref, v0_ref, low_ref, lse_ref, cos_ref, sin_ref,
    dq_ref, d2_ref, d1_ref, d0_ref, acc_ref,
):
    head, step = pl.program_id(0), pl.program_id(1)
    k_refs, v_refs = (k2_ref, k1_ref, k0_ref), (v2_ref, v1_ref, v0_ref)

    @pl.when((head == 0) & (step == 0))
    def _():
        acc_ref[...] = jnp.zeros_like(acc_ref)

    q, d_out = q_ref[...], do_ref[...]
    found = scores_of(q, k_refs, low_ref[...], step * tile, 1, 0)
    lse = lse_ref[0]
    probs = [jnp.where(ok, jnp.exp(softcap_limit * ratio - lse), 0.0) for ratio, ok in found]
    d_probs = [
        lax.dot_general(d_out, v[...], (((1,), (1,)), ((), ())), preferred_element_type=f32)
        for v in v_refs
    ]
    delta = sum(jnp.sum(p * d, axis=1, keepdims=True) for p, d in zip(probs, d_probs))
    d_query = 0.0
    for i, (p, d) in enumerate(zip(probs, d_probs)):
        ratio = found[i][0]
        d_raw = (p * (d - delta) * (1.0 - ratio * ratio) * (HEAD_DIM ** (-0.5))).astype(bf16)
        d_query += jnp.dot(d_raw, k_refs[i][...], preferred_element_type=f32)
        acc_ref[i, :, :HEAD_DIM] += contract_rows(d_raw, q)
        acc_ref[i, :, HEAD_DIM:] += contract_rows(p.astype(bf16), d_out)
    dq_ref[...] = rotate_in(d_query, cos_ref[...], -sin_ref[...]).astype(bf16)

    @pl.when((head == pl.num_programs(0) - 1) & (step == pl.num_programs(1) - 1))
    def _():
        d2_ref[...] = acc_ref[0].astype(bf16)
        d1_ref[...] = acc_ref[1].astype(bf16)
        d0_ref[...] = acc_ref[2]


def attend_back_call(query, d_out, window, low, lse, cosine, sine_tab, heads):
    rows = query.shape[0]
    tile = rows // 3
    key = pl.BlockSpec((rows, HEAD_DIM), lambda h, i: (0, 0))
    value = pl.BlockSpec((rows, HEAD_DIM), lambda h, i: (0, 1))
    mine = pl.BlockSpec((tile, HEAD_DIM), lambda h, i: (i, h))
    tab = pl.BlockSpec((tile, HEAD_DIM // 2), lambda h, i: (i, 0))
    back = pl.BlockSpec((rows, 2 * HEAD_DIM), lambda h, i: (0, 0))
    return pl.pallas_call(
        partial(attend_back_kernel, tile),
        grid=(heads, rows // tile),
        out_shape=(
            jax.ShapeDtypeStruct(query.shape, bf16),
            jax.ShapeDtypeStruct((rows, 2 * HEAD_DIM), bf16),
            jax.ShapeDtypeStruct((rows, 2 * HEAD_DIM), bf16),
            jax.ShapeDtypeStruct((rows, 2 * HEAD_DIM), f32),
        ),
        in_specs=[mine, mine]
        + [key] * 3
        + [value] * 3
        + [
            pl.BlockSpec((tile, 1), lambda h, i: (i, 0)),
            pl.BlockSpec((1, tile, 1), lambda h, i: (h, i, 0)),
            tab,
            tab,
        ],
        out_specs=(mine, back, back, back),
        scratch_shapes=[pltpu.VMEM((3, rows, 2 * HEAD_DIM), f32)],
        compiler_params=pltpu.CompilerParams(vmem_limit_bytes=56 << 20),
        cost_estimate=pl.CostEstimate(flops=ATTEND_BACK_COST, bytes_accessed=0, transcendentals=0),
        name="attend_back",
    )(query, d_out, *window, *window, low, lse, cosine, sine_tab)


def pick(array, index, axis=0):
    return lax.dynamic_index_in_dim(array, index, axis, keepdims=False)


class Order:
    def __init__(self, token):
        self.token = token

    def __call__(self, *values):
        values, self.token = lax.optimization_barrier((values, self.token))
        return values[0] if len(values) == 1 else values


def put(buffer, block, index):
    return lax.dynamic_update_index_in_dim(buffer, block, index, 0)


def local(
    inputs,
    seq_lengths,
    gain_attn_in,
    gain_attn_out,
    gain_ffn_in,
    gain_ffn_out,
    w_query,
    w_key,
    w_value,
    w_out,
    w_gate,
    w_up,
    w_down,
    out_grad,
):
    n = lax.axis_size("tok")
    m = n // 4
    width = inputs.shape[1]
    rows = inputs.shape[0]
    part = rows // 4
    tok = lax.axis_index("tok")
    tpi = lax.axis_index("tp")
    z, y = tok // m, tok % m
    zlo, zhi = z % 2, z // 2
    x, core = tpi // 2, tpi % 2
    wrows = w_query.shape[0]
    head_cols = w_query.shape[1]
    kv_cols = w_key.shape[1]
    heads = head_cols // HEAD_DIM
    kv_heads = kv_cols // HEAD_DIM
    units = w_gate.shape[1]
    half = units // 2

    def over_tok(fn):
        pairs = [(t, fn(t)) for t in range(n)]
        return lambda a: lax.ppermute(a, "tok", pairs)

    def over_tp(fn):
        pairs = [(t, fn(t)) for t in range(4)]
        return lambda a: lax.ppermute(a, "tp", pairs)

    def z_shift(a, k):
        return over_tok(lambda t: ((t // m + k) % 4) * m + t % m)(a)

    def y_shift(a, k):
        return over_tok(lambda t: (t // m) * m + (t % m + k) % m)(a)

    to_zlo = over_tok(lambda t: ((t // m) ^ 1) * m + t % m)
    to_zhi = over_tok(lambda t: ((t // m) ^ 2) * m + t % m)
    to_core = over_tp(lambda t: t ^ 1)
    to_x = over_tp(lambda t: t ^ 2)

    def within_quad(a, by):
        pairs = [(t, t + by) for t in range(n) if 0 <= t + by < n and t // QUAD == (t + by) // QUAD]
        return lax.ppermute(a, "tok", pairs)

    def place_of(dz, dy):
        return ((z ^ dz) * m) + (y - dy) % m

    step = Order(seq_lengths)

    def y_others(a):
        return [y_shift(a, j) for j in range(1, m)]

    def halves(a, index):
        return lax.dynamic_slice_in_dim(a, index * half, half, 1)

    attn_own = jnp.concatenate([w_query, w_key, w_value, w_out], axis=1)
    gains = jnp.concatenate([gain_attn_in, gain_attn_out, gain_ffn_in, gain_ffn_out])
    attn_cols = attn_own.shape[1]
    gains = jnp.pad(gains, (0, attn_cols - gains.shape[0])).reshape(1, attn_cols)
    attn_own = jnp.concatenate([attn_own, jnp.pad(gains, ((0, 15), (0, 0)))], axis=0)
    gu_keep = jnp.concatenate([halves(w_gate, zlo), halves(w_up, zlo)], axis=1)
    gu_send = jnp.concatenate([halves(w_gate, 1 - zlo), halves(w_up, 1 - zlo)], axis=1)
    d_keep, d_send = halves(w_down, zlo), halves(w_down, 1 - zlo)
    own_index = tok * rows + jnp.arange(rows, dtype=jnp.int32)
    seq_start = sequence_start(seq_lengths, own_index)
    cosine, sine_tab = rope_tables(own_index - seq_start)
    low = (seq_start - (tok - REACH) * rows)[:, None]
    attn_own, cosine, sine_tab, low = step(attn_own, cosine, sine_tab, low)
    attn_buf, gu_buf, d_buf = gather_call(n, attn_own, gu_keep, gu_send, d_keep, d_send)
    gu_z = {k: pick(gu_buf, (z ^ k) * m + y) for k in (1, 2)}
    d_z = {0: d_keep, 1: pick(d_buf, (z ^ 1) * m + y)}

    gains_all = attn_buf[:, wrows, : 4 * wrows].reshape(n, 4, wrows)
    gains_all = gains_all.transpose(1, 0, 2).reshape(4, 1, width).astype(f32)
    gain_one, gain_two, gain_three, gain_four = (gains_all[i] for i in range(4))

    def own_slice(a):
        return lax.dynamic_slice_in_dim(a, tpi * part, part, 0)

    def gather_tp(a):
        buffer = jnp.zeros((4,) + a.shape, a.dtype)
        low = a.astype(bf16)
        other = to_x(low)
        pair = to_core(jnp.stack([low, other]))
        for k, block in enumerate((a, pair[0], other, pair[1])):
            buffer = put(buffer, block.astype(a.dtype), tpi ^ k)
        return buffer.reshape((-1,) + a.shape[1:])

    def reduce_tp(compute):
        far = compute(1 - core).astype(bf16)
        near = compute(core) + to_core(far).astype(f32)
        near = near.reshape(2, part, width)
        return pick(near, x) + to_x(pick(near, 1 - x).astype(bf16)).astype(f32)

    def core_rows(a, c):
        return pick(a.reshape(2, 2, part, a.shape[1]), c, 1).reshape(2 * part, a.shape[1])

    qkv_cols = head_cols + 2 * kv_cols
    qkv_mat = attn_buf[:, :wrows, :qkv_cols].reshape(width, qkv_cols)
    out_mat = attn_buf[:, :wrows, qkv_cols:].reshape(width, head_cols)
    hidden_one, query, key_value = qkv_call(
        inputs,
        gain_one,
        attn_buf if wrows % 16 == 0 else qkv_mat[None],
        cosine,
        sine_tab,
        heads,
        kv_heads,
    )
    window = [within_quad(key_value, by) for by in range(REACH, 0, -1)] + [key_value]
    attended, lse = attend_call(query, window, low, heads, kv_heads)
    far, near = (contract_cols(core_rows(attended, c), out_mat) for c in (1 - core, core))
    def over_y(a):
        return [(a, ("y", j)) for j in range(1, m)]

    attn, gu3, *arrived = comm_call(
        n, 1, "reduce_tp", (far.astype(bf16), near), [(gu_z[1], ("zhi",))] + over_y(gu_z[1]) + over_y(gu_z[2])
    )
    gu_z[3] = gu3
    gu_y = {1: arrived[: m - 1], 2: arrived[m - 1 :]}

    resid = own_slice(inputs).astype(f32)
    unit_two, inv_two = norm_parts(attn)
    resid_mid = resid + unit_two * gain_two
    unit_three, inv_three = norm_parts(resid_mid)
    def fill(buffer, by_z, by_y):
        for k in by_z:
            buffer = put(buffer, by_z[k], (z ^ k) * m + y)
        for k in by_y:
            for j, piece in enumerate(by_y[k]):
                buffer = put(buffer, piece, (z ^ k) * m + (y - j - 1) % m)
        return buffer

    hidden_two = (unit_three * gain_three).astype(bf16)
    hidden_two, d2, d3, *arrived = comm_call(
        n,
        2,
        "gather_pair",
        (hidden_two,),
        [(d_z[0], ("zhi",)), (d_z[1], ("zhi",))] + over_y(gu_z[3]) + over_y(d_z[0]) + over_y(d_z[1]),
    )
    gu_y[3] = arrived[: m - 1]
    d_y = {0: arrived[m - 1 : 2 * m - 2], 1: arrived[2 * m - 2 :]}
    d_z[2], d_z[3] = d2, d3
    d_y[2], d_y[3] = y_others(d2), y_others(d3)
    gu_mat = fill(gu_buf, {3: gu_z[3]}, gu_y).reshape(width, -1)
    down_mat = fill(d_buf, {2: d_z[2], 3: d_z[3]}, d_y).reshape(width, -1)
    gate_up = jnp.dot(hidden_two, gu_mat, preferred_element_type=f32)
    gate_vals, up_vals = gate_up[:, :half], gate_up[:, half:]
    activated, gelu_pull = jax.vjp(partial(jax.nn.gelu, approximate=True), gate_vals)
    inner = (activated * up_vals).astype(bf16)
    inner_far, inner_near = inner[2 * rows // 2 :], inner[: 2 * rows // 2]
    (ffn,) = comm_call(
        n, 3, "reduce_pair", (contract_cols(inner_far, down_mat).astype(bf16), contract_cols(inner_near, down_mat))
    )
    unit_four, inv_four = norm_parts(ffn)
    layer_out = gather_tp((resid_mid + unit_four * gain_four).astype(bf16))

    grad_out = own_slice(out_grad).astype(f32)
    d_ffn, grad_four = norm_back(grad_out, gain_four, unit_four, inv_four)
    (d_ffn_all,) = comm_call(n, 4, "gather_pair", (d_ffn.astype(bf16),))
    d_inner = jnp.dot(d_ffn_all, down_mat, preferred_element_type=f32)

    def y_send(grad):
        blocks = grad.astype(bf16).reshape(4, m, wrows, -1)
        return [pick(blocks, y, 1)] + [y_shift(pick(blocks, (y + j) % m, 1), j) for j in range(1, m)]

    def add_up(terms):
        return sum(t.astype(f32) for t in terms)

    def zhi_send(terms):
        total = add_up(terms).reshape(2, 2, wrows, -1)
        return [pick(total, zhi), to_zhi(pick(total, 1 - zhi).astype(bf16))]

    def zlo_send(terms):
        total = add_up(terms)
        return pick(total, zlo), to_zlo(pick(total, 1 - zlo).astype(bf16)).astype(f32)

    def z_send(terms):
        total = add_up(terms)
        return [pick(total, z)] + [
            z_shift(pick(total, (z + k) % 4).astype(bf16), k) for k in range(1, 4)
        ]

    def sides(own, other):
        return jnp.where(
            zlo == 0,
            jnp.concatenate([own, other], axis=1),
            jnp.concatenate([other, own], axis=1),
        )

    down_s = y_send(contract_rows(d_ffn_all, inner))
    grad_upvals = (d_inner * activated).astype(bf16)
    grad_gatevals = gelu_pull(d_inner * up_vals)[0].astype(bf16)
    grad_gu = jnp.concatenate([grad_gatevals, grad_upvals], axis=1)
    far, near = (contract_cols(jnp.split(grad_gu, 2)[k], gu_mat) for k in (1, 0))
    near = near + to_core(far.astype(bf16)).astype(f32)
    near = near.reshape(2, 2, part, width)
    ahead_in, own_in = to_x(near[1, 1].astype(bf16)), to_x(near[1, 0].astype(bf16))
    gate_s = y_send(contract_rows(hidden_two, grad_gatevals))
    up_s = y_send(contract_rows(hidden_two, grad_upvals))
    z_in = to_zlo((near[0, 1] + ahead_in.astype(f32)).astype(bf16))
    d_hidden_two = near[0, 0] + own_in.astype(f32) + z_in.astype(f32)
    down_s = zhi_send(down_s)
    gate_s[1:] = tie(gate_s[1:], z_in)

    mid_add, grad_three = norm_back(d_hidden_two, gain_three, unit_three, inv_three)
    d_mid = grad_out + mid_add

    d_attn, grad_two = norm_back(d_mid, gain_two, unit_two, inv_two)
    d_attn_low = gather_tp(d_attn.astype(bf16))

    d_attn_low = step(d_attn_low)
    wout_s = contract_rows(d_attn_low, attended)
    d_attended = jnp.dot(d_attn_low, out_mat, preferred_element_type=f32).astype(bf16)
    gate_s, down_s = step(gate_s, down_s)
    gate_s = zhi_send(gate_s)
    d_query, *d_window, d_kv = attend_back_call(
        query, d_attended, window, low, lse, cosine, sine_tab, heads
    )
    d_window = [within_quad(d_window[REACH - by], -by) for by in range(1, REACH + 1)]
    q_grad = contract_rows(hidden_one, d_query)
    up_s, wout_s = step(up_s, wout_s)
    up_s, wout_s = zhi_send(up_s), y_send(wout_s)
    out_down = sides(*zlo_send(down_s))
    d_window = step(d_window)
    q_s = y_send(q_grad)
    d_kv = d_kv + add_up(d_window)
    d_key = rotate_in(d_kv[:, :kv_cols], cosine, -sine_tab)
    d_key_value = jnp.concatenate([d_key.astype(bf16), d_kv[:, kv_cols:].astype(bf16)], axis=1)
    d_qkv = jnp.concatenate([d_query, d_key_value], axis=1)
    kv_s = y_send(contract_rows(hidden_one, d_key_value))
    d_hidden_one = reduce_tp(lambda c: contract_cols(core_rows(d_qkv, c), qkv_mat))
    unit_one, inv_one = norm_parts(resid)
    input_add, grad_one = norm_back(d_hidden_one, gain_one, unit_one, inv_one)
    gate_s[1:] = tie(gate_s[1:], d_window)
    out_gate = sides(*zlo_send(gate_s))
    wout_s = z_send(step(wout_s))
    up_s = step(up_s)
    out_up = sides(*zlo_send(up_s))
    q_s = z_send(step(q_s))
    kv_s = z_send(step(kv_s))
    out_wout, out_q, out_kv = add_up(wout_s), add_up(q_s), add_up(kv_s)
    gain_grads = jnp.stack([grad_one, grad_two, grad_three, grad_four])
    gain_grads = gain_grads + to_core(gain_grads)
    gain_grads = gain_grads + to_x(gain_grads)
    input_grad = gather_tp(tie(d_mid + input_add, gain_grads))

    bit = 1
    while bit < n:
        gain_grads = gain_grads + over_tok(lambda t: t ^ bit)(gain_grads)
        bit *= 2
    gain_grads = lax.dynamic_slice_in_dim(gain_grads, tok * wrows, wrows, 1)
    return (
        layer_out,
        input_grad,
        gain_grads[0],
        gain_grads[1],
        gain_grads[2],
        gain_grads[3],
        out_q,
        out_kv[:, :kv_cols],
        out_kv[:, kv_cols:],
        out_wout,
        out_gate,
        out_up,
        out_down,
    )


def solution(mesh):
    weight = P("tok", "tp")
    in_specs = (P("tok", None), P()) + (P("tok"),) * 4 + (weight,) * 7 + (P("tok", None),)
    out_specs = (P("tok", None),) * 2 + (P("tok"),) * 4 + (weight,) * 7
    return jax.shard_map(local, mesh=mesh, in_specs=in_specs, out_specs=out_specs, check_vma=False)
```
